32 devices in a mesh: rep: 4 (over y, core), shard: 8 (over z, x).
Axes of the slice: x: 2, y: 2, z: 4, core: 2. Of those that a mesh axis runs over, the one named last changes fastest.
Arguments:
- tokens: bfloat16 [32768, 1024], P(('rep', 'shard')), may hold values from -6 to 6
- doc_lengths: int32 [32, 4], P(('rep', 'shard')), may hold values from 1 to 512, 1024 in all within a row
- cotangent: bfloat16 [32768, 1024], P(('rep', 'shard')), may hold values from -6 to 6
- qkv_weight: float32 [1024, 3072], P('shard'), may hold values from -0.125 to 0.125
- qkv_firsts: float32 [1024, 3072], P('shard'), may hold values from -0.00048828125 to 0.00048828125
- qkv_seconds: float32 [1024, 3072], P('shard'), may hold values from 2.0644464e-09 to 3.3348748e-08
- dense_weight: float32 [1024, 1024], P('shard'), may hold values from -0.75 to 0.75
- dense_firsts: float32 [1024, 1024], P('shard'), may hold values from -0.00048828125 to 0.00048828125
- dense_seconds: float32 [1024, 1024], P('shard'), may hold values from 2.0644464e-09 to 3.3348748e-08
- expand_weight: float32 [1024, 4096], P('shard'), may hold values from -0.1875 to 0.1875
- expand_firsts: float32 [1024, 4096], P('shard'), may hold values from -0.00048828125 to 0.00048828125
- expand_seconds: float32 [1024, 4096], P('shard'), may hold values from 2.0644464e-09 to 3.3348748e-08
- shrink_weight: float32 [4096, 1024], P('shard'), may hold values from -0.09375 to 0.09375
- shrink_firsts: float32 [4096, 1024], P('shard'), may hold values from -0.00048828125 to 0.00048828125
- shrink_seconds: float32 [4096, 1024], P('shard'), may hold values from 2.0644464e-09 to 3.3348748e-08
- vectors: float32 [1024, 11], P('shard'), may hold values from -1.5 to 2.64
- vec_firsts: float32 [1024, 11], P('shard'), may hold values from -0.00048828125 to 0.00048828125
- vec_seconds: float32 [1024, 11], P('shard'), may hold values from 2.0644464e-09 to 3.3348748e-08
Outputs:
- out: bfloat16 [32768, 1024], P(('rep', 'shard'))
- grad_in: float32 [32768, 1024], P(('rep', 'shard'))
- qkv_momentum: float32 [1024, 3072], P('shard')
- qkv_variance: float32 [1024, 3072], P('shard')
- qkv_renewed: float32 [1024, 3072], P('shard')
- dense_momentum: float32 [1024, 1024], P('shard')
- dense_variance: float32 [1024, 1024], P('shard')
- dense_renewed: float32 [1024, 1024], P('shard')
- expand_momentum: float32 [1024, 4096], P('shard')
- expand_variance: float32 [1024, 4096], P('shard')
- expand_renewed: float32 [1024, 4096], P('shard')
- shrink_momentum: float32 [4096, 1024], P('shard')
- shrink_variance: float32 [4096, 1024], P('shard')
- shrink_renewed: float32 [4096, 1024], P('shard')
- vec_momentum: float32 [1024, 11], P('shard')
- vec_variance: float32 [1024, 11], P('shard')
- vec_renewed: float32 [1024, 11], P('shard')
- grad_norm: float32 [1], replicated
The draws below stay inside these ranges and needn't reach their ends.
Inputs may be any that keep to these rules, and one draw needn't show every extreme that they name: `doc_lengths`: row r holds, in order, the lengths of the 4 documents packed into sequence r; each row sums to 1024.
All inputs are finite; a program needn't handle non-finite values.
Results may differ from the reference program's by a relative error of at most 0.02.
Values may be sent and summed in bfloat16 or wider, within the bound.
A program may use at most 384 MiB of HBM per device.

```python
import math
import jax
import jax.numpy as jnp
import numpy as np
from jax import lax

D = 1024
HEADS = 16
HEAD_DIM = 64
ROTARY = 32
FF = 4096
LEN = 1024
DOCS = 4
STEP = 10
SEQS = 32
TOKENS = 32768
VROWS = 11
PARAMS = 12594176


def draw_vectors(key, part):
    key = jax.random.fold_in(key, 7)
    ramp_key, rest_key = jax.random.split(key)
    fraction = jnp.arange(D, dtype=jnp.float32) / (D - 1)
    jitter = jax.random.uniform(ramp_key, (D,), jnp.float32, 0.9, 1.1)
    ramp_values = 1.0 + fraction
    others = jnp.clip(0.3 * jax.random.normal(rest_key, (D, VROWS - 1), jnp.float32), -1.5, 1.5)
    return jnp.concatenate([(ramp_values * jitter)[:, None], others], axis=1)


def block_scale(stream_key, dims, cuts, least, high):
    def one(axis_at, blocks):
        steps = jax.random.uniform(jax.random.fold_in(jax.random.fold_in(stream_key, 6), axis_at), (blocks,), jnp.float32, least / len(cuts), high / len(cuts))
        return jnp.repeat(jnp.exp(steps), dims[axis_at] // blocks).reshape((-1,) + (1,) * (len(dims) - axis_at - 1))

    factor_of = one(*cuts[0])
    for cut in cuts[1:]:
        factor_of = factor_of * one(*cut)
    return factor_of


def length_profile(count, total, reach, lean):
    loads = [(1 << 20) // math.isqrt(rank ** lean) + 1 for rank in range(2, count + 1)]
    surplus, holding = total - reach - (count - 1), [1] * (count - 1)
    while surplus > 0:
        candidates = [i for i in range(count - 1) if holding[i] < reach]
        mass, left = sum([loads[i] for i in candidates]), surplus
        for i in candidates:
            more = min(reach - holding[i], max(1, left * loads[i] // mass), surplus)
            holding[i] = holding[i] + more
            surplus = surplus - more
    return np.array([reach] + holding)


def uneven(rng, count, total, limit, slope):
    if count == 2:
        one = jax.random.randint(rng, (), max(1, total - limit), min(limit, total - 1) + 1)
        return jnp.stack([one, total - one])
    lengths = jnp.asarray(length_profile(count, total, limit, slope), jnp.int32)
    couples = (count - 1) // 2
    source_of, receiver = lengths[1:1 + 2 * couples:2], lengths[2:2 + 2 * couples:2]
    room = jnp.minimum(source_of - 1, limit - receiver)
    shifted = jax.random.randint(jax.random.fold_in(rng, 1), (couples,), 0, 1 << 20) % (room + 1)
    lengths = lengths.at[1:1 + 2 * couples:2].set(source_of - shifted).at[2:2 + 2 * couples:2].set(receiver + shifted)
    return lengths[jax.random.permutation(jax.random.fold_in(rng, 2), count)]


def centred(stream_key, dims, deviation, most, cuts=(), kind=jnp.bfloat16):
    factor_of = block_scale(stream_key, dims, cuts, -0.22, 0.18) if cuts else 1.0
    array = jax.random.normal(stream_key, dims, jnp.float32) * deviation * factor_of
    return jnp.minimum(jnp.maximum(array, -most), most).astype(kind)


def setup_inputs(seed: int = 0) -> dict:
    splits = jax.random.split(jax.random.key(seed), 19)
    return {
        "tokens": centred(splits[0], (TOKENS, D), 1.0, 6.0, ((0, 32),)),
        "doc_lengths": jax.vmap(lambda own: uneven(own, DOCS, LEN, LEN // 2, 2))(jax.random.split(splits[1], SEQS)).reshape((SEQS, DOCS)).astype(jnp.int32),
        "cotangent": centred(splits[2], (TOKENS, D), 1.0, 6.0, ((0, 32),)),
        "qkv_weight": centred(splits[3], (D, 3 * D), (2 * D) ** -0.5, 0.125, ((0, 8),), jnp.float32),
        "qkv_firsts": centred(splits[4], (D, 3 * D), (0.111 * PARAMS ** -0.5), 0.00048828125, ((0, 8),), jnp.float32),
        "qkv_seconds": jnp.clip(jnp.exp(math.log(3.3348747763284337e-08) - 2.7821581 * jax.random.uniform(splits[5], (D, 3 * D), jnp.float32) ** block_scale(splits[5], (D, 3 * D), ((0, 8),), -0.2, 0.2)), 2.064446391614183e-09, 3.3348747763284337e-08),
        "dense_weight": centred(splits[6], (D, D), (D // 16) ** -0.5, 0.75, ((0, 8),), jnp.float32),
        "dense_firsts": centred(splits[7], (D, D), (0.111 * PARAMS ** -0.5), 0.00048828125, ((0, 8),), jnp.float32),
        "dense_seconds": jnp.clip(jnp.exp(math.log(3.3348747763284337e-08) - 2.7821581 * jax.random.uniform(splits[8], (D, D), jnp.float32) ** block_scale(splits[8], (D, D), ((0, 8),), -0.2, 0.2)), 2.064446391614183e-09, 3.3348747763284337e-08),
        "expand_weight": centred(splits[9], (D, FF), D ** -0.5, 0.1875, ((0, 8),), jnp.float32),
        "expand_firsts": centred(splits[10], (D, FF), (0.111 * PARAMS ** -0.5), 0.00048828125, ((0, 8),), jnp.float32),
        "expand_seconds": jnp.clip(jnp.exp(math.log(3.3348747763284337e-08) - 2.7821581 * jax.random.uniform(splits[11], (D, FF), jnp.float32) ** block_scale(splits[11], (D, FF), ((0, 8),), -0.2, 0.2)), 2.064446391614183e-09, 3.3348747763284337e-08),
        "shrink_weight": centred(splits[12], (FF, D), FF ** -0.5, 0.09375, ((0, 8),), jnp.float32),
        "shrink_firsts": centred(splits[13], (FF, D), (0.111 * PARAMS ** -0.5), 0.00048828125, ((0, 8),), jnp.float32),
        "shrink_seconds": jnp.clip(jnp.exp(math.log(3.3348747763284337e-08) - 2.7821581 * jax.random.uniform(splits[14], (FF, D), jnp.float32) ** block_scale(splits[14], (FF, D), ((0, 8),), -0.2, 0.2)), 2.064446391614183e-09, 3.3348747763284337e-08),
        "vectors": draw_vectors(jax.random.fold_in(splits[18], 71), 0),
        "vec_firsts": centred(splits[16], (D, VROWS), (0.111 * PARAMS ** -0.5), 0.00048828125, ((0, 8),), jnp.float32),
        "vec_seconds": jnp.clip(jnp.exp(math.log(3.3348747763284337e-08) - 2.7821581 * jax.random.uniform(splits[17], (D, VROWS), jnp.float32) ** block_scale(splits[17], (D, VROWS), ((0, 8),), -0.2, 0.2)), 2.064446391614183e-09, 3.3348747763284337e-08),
    }


highest = lax.Precision.HIGHEST
clip_limit = 1.0
matrix_rate = 0.05
vector_rate = 0.8
decay_rate = 0.1

@jax.custom_vjp
def low(v):
    return lax.optimization_barrier(v.astype(jnp.bfloat16)).astype(jnp.float32)

@jax.custom_vjp
def low_back(v):
    return v

def low_keep(v):
    return (low(v), None)

def low_pass(kept, grad):
    return (grad,)

def back_keep(v):
    return (v, None)

def back_low(kept, grad):
    return (low(grad),)
low.defvjp(low_keep, low_pass)
low_back.defvjp(back_keep, back_low)

def doc_layout(lengths_rows):
    ends = jnp.cumsum(lengths_rows, axis=-1).astype(jnp.int32)
    places = jnp.arange(LEN, dtype=jnp.int32)
    passed = (places[None, :, None] >= ends[:, None, :]).astype(jnp.int32)
    doc_ids = lax.optimization_barrier(jnp.sum(passed, axis=-1)).astype(jnp.int32)
    starts = lax.optimization_barrier(jnp.sum(passed * lengths_rows[:, None, :], axis=-1)).astype(jnp.int32)
    return (doc_ids, (places[None, :] - starts).astype(jnp.int32))

def rotary_tables(positions):
    exponent = jnp.arange(0, ROTARY, 2, dtype=jnp.float32) / ROTARY
    frequency = 10000.0 ** (-exponent)
    angles = positions.astype(jnp.float32)[:, None] * frequency[None, :]
    cosine = jnp.concatenate([jnp.cos(angles), jnp.cos(angles)], axis=-1)[:, None, :]
    sine_part = jnp.concatenate([jnp.sin(angles), jnp.sin(angles)], axis=-1)[:, None, :]
    return (cosine, sine_part)

def rotate(heads, cosine, sine_part):
    half_dim = ROTARY // 2
    turned = heads[..., :ROTARY]
    swapped = jnp.concatenate([-turned[..., half_dim:], turned[..., :half_dim]], axis=-1)
    return jnp.concatenate([turned * cosine + swapped * sine_part, heads[..., ROTARY:]], axis=-1)

def attend_block(query_rows, key_rows, value_rows, doc_query, doc_key, index_query, index_key):
    scores = low_back(jnp.einsum('qhd,khd->hqk', query_rows, key_rows, precision=highest))
    allowed = (doc_query[:, None] == doc_key[None, :]) & (index_key[None, :] <= index_query[:, None])
    scores = jnp.where(allowed[None], scores, -1e+30)
    top_score = lax.optimization_barrier(jnp.max(scores, axis=-1, keepdims=True))
    weights = jnp.exp(scores - top_score)
    probs = weights / lax.optimization_barrier(jnp.sum(weights, axis=-1, keepdims=True))
    return jnp.einsum('hqk,khd->qhd', low(probs), value_rows, precision=highest)

def attention(queries, keys_rot, values, doc_ids):
    block_rows = min(512, LEN)
    block_count = LEN // block_rows
    index_all = jnp.arange(LEN, dtype=jnp.int32)

    def one_sequence(pack):
        seq_queries, seq_keys, seq_values, seq_docs = pack

        def one_block(block_pack):
            return attend_block(block_pack[0], seq_keys, seq_values, block_pack[1], seq_docs, block_pack[2], index_all)
        blocks = (seq_queries.reshape(block_count, block_rows, HEADS, HEAD_DIM), seq_docs.reshape(block_count, block_rows), index_all.reshape(block_count, block_rows))
        return lax.map(jax.checkpoint(one_block), blocks).reshape(LEN, HEADS, HEAD_DIM)
    return lax.map(one_sequence, (queries, keys_rot, values, doc_ids))

def layer_forward(params, inputs, doc_ids, positions):
    vectors, qkv_weight, dense_weight, expand_weight, shrink_weight = params
    table = low(vectors)
    expand_ratio = FF // D
    ln_gain = table[:, 0]
    ln_shift = table[:, 1]
    qkv_bias = table[:, 2:5].T.reshape(3 * D)
    dense_bias = table[:, 5]
    expand_bias = table[:, 6:6 + expand_ratio].T.reshape(FF)
    shrink_bias = table[:, VROWS - 1]
    centered = inputs - lax.optimization_barrier(jnp.mean(inputs, axis=-1, keepdims=True))
    scaled = centered * lax.rsqrt(lax.optimization_barrier(jnp.mean(centered * centered, axis=-1, keepdims=True)) + 1e-05)
    normed = low(scaled * ln_gain + ln_shift)
    mixed = low_back(jnp.dot(normed, low(qkv_weight), precision=highest, preferred_element_type=jnp.float32) + qkv_bias)
    token_count = inputs.shape[0]
    seq_count = token_count // LEN
    cosine, sine_part = rotary_tables(positions.reshape(token_count))
    head_shape = (token_count, HEADS, HEAD_DIM)
    queries = low(rotate(mixed[:, :D].reshape(head_shape), cosine, sine_part) / math.sqrt(HEAD_DIM))
    keys_rot = low(rotate(mixed[:, D:2 * D].reshape(head_shape), cosine, sine_part))
    values = low(mixed[:, 2 * D:].reshape(head_shape))
    seq_shape = (seq_count, LEN, HEADS, HEAD_DIM)
    attended = attention(queries.reshape(seq_shape), keys_rot.reshape(seq_shape), values.reshape(seq_shape), doc_ids)
    attended = low(low_back(attended.reshape(token_count, D)))
    branch_attn = jnp.dot(attended, low(dense_weight), precision=highest, preferred_element_type=jnp.float32) + dense_bias
    pre_act = low_back(jnp.dot(normed, low(expand_weight), precision=highest, preferred_element_type=jnp.float32) + expand_bias)
    activated = low(jax.nn.gelu(pre_act, approximate=True))
    branch_mlp = jnp.dot(activated, low(shrink_weight), precision=highest, preferred_element_type=jnp.float32) + shrink_bias
    return inputs + branch_attn + branch_mlp

def adamw(master, firsts, seconds, gradient, factor, step_rate, decay_amount):
    clipped = gradient * factor
    momentum = 0.9 * firsts + 0.1 * clipped
    variance = 0.95 * seconds + 0.05 * clipped * clipped
    corrected = momentum / (1.0 - 0.9 ** STEP)
    spread = variance / (1.0 - 0.95 ** STEP)
    renewed = master - step_rate * (corrected / (jnp.sqrt(spread) + 1e-08) + decay_amount * master)
    return (momentum, variance, renewed)

def reference(tokens, doc_lengths, cotangent, qkv_weight, qkv_firsts, qkv_seconds, dense_weight, dense_firsts, dense_seconds, expand_weight, expand_firsts, expand_seconds, shrink_weight, shrink_firsts, shrink_seconds, vectors, vec_firsts, vec_seconds):
    group = math.gcd(SEQS, max(1, 4096 // LEN))
    steps_count = SEQS // group
    doc_ids, positions = doc_layout(doc_lengths)
    inputs = tokens.astype(jnp.float32).reshape(steps_count, group * LEN, D)
    backs = cotangent.astype(jnp.float32).reshape(steps_count, group * LEN, D)
    doc_ids = doc_ids.reshape(steps_count, group, LEN)
    positions = positions.reshape(steps_count, group, LEN)
    params = (vectors, qkv_weight, dense_weight, expand_weight, shrink_weight)
    zero_grads = jax.tree.map(jnp.zeros_like, params)

    def one_step(totals, pack):
        piece, back, piece_docs, piece_pos = pack
        result, pullback = jax.vjp(lambda p_all, x_all: layer_forward(p_all, x_all, piece_docs, piece_pos), params, piece)
        grads_params, grad_inputs = pullback(back)
        return (jax.tree.map(jnp.add, totals, grads_params), (result.astype(jnp.bfloat16), grad_inputs))
    totals, (outputs, grad_inputs) = lax.scan(one_step, zero_grads, (inputs, backs, doc_ids, positions))
    grad_table, grad_qkv, grad_dense, grad_expand, grad_shrink = totals
    squares = sum((jnp.sum(gradient * gradient) for gradient in totals))
    grad_norm = jnp.sqrt(squares)
    factor = jnp.minimum(1.0, clip_limit / (grad_norm + 1e-06))
    qkv_new = adamw(qkv_weight, qkv_firsts, qkv_seconds, grad_qkv, factor, matrix_rate, decay_rate)
    dense_new = adamw(dense_weight, dense_firsts, dense_seconds, grad_dense, factor, matrix_rate, decay_rate)
    expand_new = adamw(expand_weight, expand_firsts, expand_seconds, grad_expand, factor, matrix_rate, decay_rate)
    shrink_new = adamw(shrink_weight, shrink_firsts, shrink_seconds, grad_shrink, factor, matrix_rate, decay_rate)
    vec_new = adamw(vectors, vec_firsts, vec_seconds, grad_table, factor, vector_rate, 0.0)
    return (outputs.reshape(TOKENS, D), grad_inputs.reshape(TOKENS, D), qkv_new[0], qkv_new[1], qkv_new[2], dense_new[0], dense_new[1], dense_new[2], expand_new[0], expand_new[1], expand_new[2], shrink_new[0], shrink_new[1], shrink_new[2], vec_new[0], vec_new[1], vec_new[2], grad_norm.reshape(1))
```

```python
import math

import jax
import jax.numpy as jnp
from jax import lax
from jax.experimental import pallas as pl
from jax.experimental.pallas import tpu as pltpu
from jax.sharding import PartitionSpec as P

D = 1024
HEADS = 16
HEAD_DIM = 64
ROTARY = 32
FF = 4096
LEN = 1024
STEP = 10
VROWS = 11
VPAD = 16
UNITS = 12
QB = 256

clip_limit = 1.0
matrix_rate = 0.05
vector_rate = 0.8
decay_rate = 0.1

BF = jnp.bfloat16
F32 = jnp.float32
MIB = 1 << 20


def dot(a, b, ca, cb):
    return lax.dot_general(a, b, (((ca,), (cb,)), ((), ())), preferred_element_type=F32)


class Place:
    def __init__(self, nz):
        self.nz = nz
        self.r = lax.axis_index("rep")
        self.s = lax.axis_index("shard")
        self.z, self.x = self.s // 2, self.s % 2
        self.c = self.r % 2
        self.y = (self.r // 2) % 2
        self.p = 2 * self.c + self.y

    def dev(self, r, s):
        return {"rep": r, "shard": s}

    def zpeer(self, k):
        return self.dev(self.r, ((self.z + k) % self.nz) * 2 + self.x)

    @property
    def xpeer(self):
        return self.dev(self.r, self.z * 2 + 1 - self.x)

    @property
    def ypeer(self):
        return self.dev(self.r + 2 - 4 * self.y, self.s)

    @property
    def cpeer(self):
        return self.dev(self.r + 1 - 2 * self.c, self.s)

    @property
    def diag(self):
        return self.dev(self.r + 2 - 4 * self.y + 1 - 2 * self.c, self.s)

    def swap(self, first):
        on_x = self.c == (0 if first else 1)
        return self.dev(
            jnp.where(on_x, self.r, self.r + 2 - 4 * self.y),
            jnp.where(on_x, self.z * 2 + 1 - self.x, self.s),
        )


def greet(peers):
    barrier = pltpu.get_barrier_semaphore()
    for peer in peers:
        pl.semaphore_signal(barrier, inc=1, device_id=peer, device_id_type=pl.DeviceIdType.MESH)
    pl.semaphore_wait(barrier, len(peers))


def remote(src, dst, send, recv, peer):
    return pltpu.make_async_remote_copy(
        src_ref=src,
        dst_ref=dst,
        send_sem=send,
        recv_sem=recv,
        device_id=peer,
        device_id_type=pl.DeviceIdType.MESH,
    )


class Gather:
    def __init__(self, at, own, full, u0, n, send, recv, base):
        self.at, self.own, self.full = at, own, full
        self.us = pl.ds(u0, n)
        self.send, self.recv, self.base = send, recv, base

    @staticmethod
    def sems(nz):
        return (nz - 1) + nz + 2 * nz + 2 * nz

    def block(self, k, other):
        at = self.at
        zk = (at.z + at.nz - k) % at.nz
        return zk * 2 + (1 - at.x if other else at.x)

    def copy(self, sem, src, dst, peer):
        i = self.base + sem
        return remote(src, dst, self.send.at[i], self.recv.at[i], peer)

    def rows(self, y):
        return pl.ds(self.at.c * 64 + y * 32, 32)

    def mine(self, k):
        return self.own.at[self.us, self.rows(self.at.y)] if k == 0 else self.full.at[
            self.us, self.block(k, False), self.rows(self.at.y)
        ]

    def send_z(self, k):
        dst = self.full.at[self.us, self.at.s, self.rows(self.at.y)]
        return self.copy(k - 1, self.mine(0), dst, self.at.zpeer(k))

    def recv_z(self, k):
        dst = self.full.at[self.us, self.block(k, False), self.rows(self.at.y)]
        return self.copy(k - 1, self.mine(0), dst, self.at.zpeer(k))

    def place_a(self, k):
        at = self.at
        zk = (at.z + at.nz - k) % at.nz
        block = zk * 2 + jnp.where(at.c == 0, 1 - at.x, at.x)
        return self.full.at[self.us, block, self.rows(jnp.where(at.c == 0, at.y, 1 - at.y))]

    def send_a(self, k):
        dst = self.full.at[self.us, self.block(k, False), self.rows(self.at.y)]
        return self.copy(self.at.nz - 1 + k, self.mine(k), dst, self.at.swap(True))

    def recv_a(self, k):
        return self.copy(self.at.nz - 1 + k, self.mine(k), self.place_a(k), self.at.swap(True))

    def send_b(self, k, j):
        i = 2 * self.at.nz - 1 + 2 * k + j
        if j == 0:
            dst = self.full.at[self.us, self.block(k, False), self.rows(self.at.y)]
            return self.copy(i, self.mine(k), dst, self.at.swap(False))
        return self.copy(i, self.place_a(k), self.place_a(k), self.at.swap(False))

    def own_b(self):
        src = self.own.at[self.us, self.rows(1 - self.at.y)]
        return self.copy(2 * self.at.nz, src, self.place_a(0), self.at.swap(False))

    def recv_b(self, k, j):
        at = self.at
        i = 2 * at.nz - 1 + 2 * k + j
        zk = (at.z + at.nz - k) % at.nz
        if j == 0:
            block = zk * 2 + jnp.where(at.c == 0, at.x, 1 - at.x)
            dst = self.full.at[self.us, block, self.rows(jnp.where(at.c == 0, 1 - at.y, at.y))]
        else:
            dst = self.full.at[self.us, zk * 2 + 1 - at.x, self.rows(1 - at.y)]
        return self.copy(i, dst, dst, at.swap(False))

    def send_c(self, k, other):
        i = 4 * self.at.nz - 1 + 2 * k + other
        ref = self.full.at[self.us, self.block(k, other), pl.ds(self.at.c * 64, 64)]
        return self.copy(i, ref, ref, self.at.cpeer)

    def recv_c(self, k, other):
        i = 4 * self.at.nz - 1 + 2 * k + other
        ref = self.full.at[self.us, self.block(k, other), pl.ds((1 - self.at.c) * 64, 64)]
        return self.copy(i, ref, ref, self.at.cpeer)

    def only(self, core, what):
        pl.when(self.at.c == core)(what)

    def stage0(self):
        for k in range(1, self.at.nz):
            self.send_z(k).start()
        self.only(0, lambda: self.send_a(0).start())
        self.only(1, lambda: self.send_b(0, 0).start())

    def stage1(self):
        for k in range(1, self.at.nz):
            self.recv_z(k).wait_recv()
            self.send_a(k).start()
            self.send_b(k, 0).start()

    def stage2(self):
        for k in range(self.at.nz):
            if k == 0:
                self.only(0, lambda: self.recv_a(0).wait_recv())
                self.only(0, lambda: self.send_b(0, 1).start())
                self.only(1, lambda: self.own_b().start())
            else:
                self.recv_a(k).wait_recv()
                self.send_b(k, 1).start()

    def stage3(self):
        for k in range(self.at.nz):
            if k == 0:
                self.only(1, lambda: self.recv_b(0, 0).wait_recv())
            else:
                self.recv_b(k, 0).wait_recv()
                self.send_c(k, 0).start()
            self.recv_b(k, 1).wait_recv()
            self.send_c(k, 1).start()

    def stage4(self):
        for k in range(self.at.nz):
            if k:
                self.recv_c(k, 0).wait_recv()
            self.recv_c(k, 1).wait_recv()
        for k in range(1, self.at.nz):
            self.send_z(k).wait_send()
        for k in range(self.at.nz):
            if k:
                self.send_a(k).wait_send()
                self.send_b(k, 0).wait_send()
                self.send_c(k, 0).wait_send()
            else:
                self.only(0, lambda: self.send_a(0).wait_send())
                self.only(1, lambda: self.send_b(0, 0).wait_send())
            self.send_b(k, 1).wait_send()
            self.send_c(k, 1).wait_send()


def rotate_rows(u, cosine, sine):
    top = u[:16] * cosine - u[16:32] * sine
    low = u[16:32] * cosine + u[:16] * sine
    return jnp.concatenate([top, low, u[32:]], axis=0)


def head_attention(rows, outs, bias, qt, kt, vt, gt, act, dqt, dkt, dvt):
    for number in range(LEN // QB):
        q0 = number * QB
        k0 = max(0, number - 2) * QB
        span = q0 + QB - k0
        q = qt[rows, q0 : q0 + QB]
        g = gt[rows, q0 : q0 + QB]
        k = kt[rows, k0 : k0 + span]
        v = vt[rows, k0 : k0 + span]
        s = dot(k, q, 0, 0) + bias[number, :span]
        e = jnp.exp(s - jnp.max(s, axis=0, keepdims=True))
        p = e * (1.0 / jnp.sum(e, axis=0, keepdims=True))
        pb = p.astype(BF)
        o = dot(v, pb, 1, 0)
        dp = dot(v, g, 0, 0)
        inner = jnp.sum(o * g.astype(F32), axis=0, keepdims=True)
        ds = (p * (dp - inner)).astype(BF)
        act[0, outs, q0 : q0 + QB] = o.astype(BF)
        dqt[:, q0 : q0 + QB] = dot(k, ds, 1, 0)
        dk = dot(q, ds, 1, 1)
        dv = dot(g, pb, 1, 1)
        old = span - QB
        if old:
            dkt[:, k0 : k0 + old] += dk[:, :old]
            dvt[:, k0 : k0 + old] += dv[:, :old]
        dkt[:, q0 : q0 + QB] = dk[:, old:]
        dvt[:, q0 : q0 + QB] = dv[:, old:]


class GatherGroup(Gather):
    def __init__(self, at, own, full, u0, n, send, recv, row):
        super().__init__(at, own, full, u0, n, send, recv, 0)
        self.row = row

    def copy(self, sem, src, dst, peer):
        return remote(src, dst, self.send.at[self.row, sem], self.recv.at[self.row, sem], peer)


def run_stage(gather, stage):
    getattr(gather, f"stage{stage}")()


def front_kernel(
    nz,
    lengths, tokens, dy, wqkv, wd, vec, wexpand, wshrink,
    full, table, ht, act,
    own, expand_f, shrink_f, weights, bias, cosine, sine, qt, kt, vt, gt, dqf, dkf, dvf,
    send_a, recv_a, send_f, recv_f, vsend, vrecv, lsem,
):
    at = Place(nz)
    shards = 2 * nz
    others = [at.dev(at.r, (at.s + k) % shards) for k in range(1, shards)]
    load_expand = pltpu.make_async_copy(wexpand, expand_f, lsem.at[0])
    load_shrink = pltpu.make_async_copy(wshrink, shrink_f, lsem.at[1])
    load_expand.start()
    load_shrink.start()
    own[0] = wd[...].astype(BF)
    for i in range(3):
        own[1 + i] = wqkv[:, i * D : i * D + D].astype(BF)
    greet(others + [at.ypeer, at.cpeer])

    def lanes(i):
        return pl.ds(pl.multiple_of(i * 128, 128), 128)

    vcopies = [
        remote(vec, table.at[:, lanes(at.s)], vsend.at[k], vrecv.at[k], peer)
        for k, peer in enumerate(others)
    ]
    for copy in vcopies:
        copy.start()
    table[:, lanes(at.s)] = vec[...]
    local_a = pltpu.make_async_copy(own.at[0:4], full.at[0:4, at.s], lsem.at[2])
    local_a.start()
    first = [GatherGroup(at, own, full, u, 1, send_a, recv_a, u) for u in range(4)]
    local_f = pltpu.make_async_copy(own.at[4:UNITS], full.at[4:UNITS, at.s], lsem.at[3])

    def cast_rest():
        load_expand.wait()
        load_shrink.wait()
        width = FF // shards
        for j in range(FF // D):
            own[4 + 2 * j] = shrink_f[j * 128 : j * 128 + 128].astype(BF)
            for b in range(shards):
                own[5 + 2 * j, :, b * 128 : b * 128 + 128] = expand_f[
                    :, b * width + j * 128 : b * width + j * 128 + 128
                ].astype(BF)
        local_f.start()

    def tables():
        place = lax.broadcasted_iota(jnp.int32, (1, LEN), 1)
        start = jnp.zeros((1, LEN), jnp.int32)
        end = 0
        for d in range(lengths.shape[1]):
            end = end + lengths[0, d]
            start = start + jnp.where(place >= end, lengths[0, d], 0)
        m = lax.broadcasted_iota(jnp.int32, (ROTARY // 2, LEN), 0).astype(F32)
        frequency = jnp.exp(m * (-2.0 * math.log(10000.0) / ROTARY))
        angle = (place - start).astype(F32) * frequency
        cosine[...] = jnp.cos(angle)
        sine[...] = jnp.sin(angle)
        for number in range(LEN // QB):
            q0 = number * QB
            k0 = max(0, number - 2) * QB
            span = q0 + QB - k0
            j = k0 + lax.broadcasted_iota(jnp.int32, (span, QB), 0)
            i = q0 + lax.broadcasted_iota(jnp.int32, (span, QB), 1)
            allowed = (j >= start[:, q0 : q0 + QB]) & (j <= i)
            bias[number, :span] = jnp.where(allowed, 0.0, -1e30)

    def wait_vec():
        for k, copy in enumerate(vcopies):
            came = (at.s + shards - (k + 1)) % shards
            remote(vec, table.at[:, lanes(came)], vsend.at[k], vrecv.at[k], others[k]).wait_recv()
            copy.wait_send()

    def norm_rows(i):
        rows = pl.ds(pl.multiple_of(i * 256, 256), 256)
        x = tokens[rows].astype(F32)
        centered = x - jnp.mean(x, axis=1, keepdims=True)
        scaled = centered * lax.rsqrt(jnp.mean(centered * centered, axis=1, keepdims=True) + 1e-05)
        h = scaled * table[0:1].astype(F32) + table[1:2].astype(F32)
        ht[:, rows] = h.astype(BF).T

    side = {0: cast_rest, 1: tables, 2: wait_vec}
    for i in range(4):
        side[3 + i] = lambda i=i: norm_rows(i)

    def later_step(t):
        for stage in range(5):
            g = t - stage

            def go(g=g, stage=stage):
                run_stage(GatherGroup(at, own, full, 4 + 2 * g, 2, send_f, recv_f, g), stage)

            if isinstance(g, int):
                if 0 <= g < 4:
                    go()
            else:
                pl.when((g >= 0) & (g < 4))(go)

    def load_weights(u):
        return pltpu.make_async_copy(full.at[u], weights.at[u], lsem.at[4 + u])

    for step in range(8):
        for stage in range(5):
            if 0 <= step - stage < 4:
                run_stage(first[step - stage], stage)
                if stage == 4:
                    if step == 4:
                        local_a.wait()
                    load_weights(step - stage).start()
        if step in side:
            side[step]()
        if step == 5:
            later_step(0)
        if step == 7:
            later_step(1)
    for u in range(4):
        load_weights(u).wait()

    def prepare(quad):
        cols = pl.ds(pl.multiple_of(quad * 256, 256), 256)
        for part, dst in enumerate((qt, kt, vt)):
            w = weights[1 + part, :, :, cols].reshape(D, 256)
            u = dot(w, ht[...], 0, 0)
            ones = jnp.ones((1, 128), BF)
            b = dot(table[2 + part : 3 + part, cols], ones, 0, 0)[:, :1]
            u = u + b
            if part == 2:
                dst[...] = u.astype(BF)
                continue
            for head in range(4):
                turned = rotate_rows(u[head * 64 : head * 64 + 64], cosine[...], sine[...])
                if part == 0:
                    turned = turned * (1.0 / math.sqrt(HEAD_DIM))
                dst[head * 64 : head * 64 + 64] = turned.astype(BF)
        for half in range(2):
            w = weights[0, 2 * quad + half]
            gt[half * 128 : half * 128 + 128] = dot(w, dy[...], 1, 1).astype(BF)

    def one_head(number, carry):
        quad, head = number // 4, number % 4
        pl.when(head == 0)(lambda: prepare(quad))
        rows = pl.ds(pl.multiple_of(head * 64, 64), 64)
        outs = pl.ds(pl.multiple_of(number * 64, 64), 64)
        head_attention(rows, outs, bias, qt, kt, vt, gt, act, dqf, dkf, dvf)
        back = rotate_rows(dqf[...], cosine[...], -sine[...]) * (1.0 / math.sqrt(HEAD_DIM))
        act[1, outs] = back.astype(BF)
        act[2, outs] = rotate_rows(dkf[...], cosine[...], -sine[...]).astype(BF)
        act[3, outs] = dvf[...].astype(BF)
        t = 2 + number // 2
        pl.when((number % 2 == 1) & (t < 8))(lambda: later_step(t))
        return carry

    lax.fori_loop(0, HEADS, one_head, 0)
    local_f.wait()


def front(lengths, tokens, dy, wqkv, wd, vec, wexpand, wshrink, nz):
    shards = 2 * nz
    count = Gather.sems(nz)
    anywhere = pl.BlockSpec(memory_space=pl.ANY)
    inside = pl.BlockSpec(memory_space=pltpu.VMEM)

    def kernel(*refs):
        front_kernel(nz, *refs)

    return pl.pallas_call(
        kernel,
        out_shape=(
            jax.ShapeDtypeStruct((UNITS, shards, 128, D), BF),
            jax.ShapeDtypeStruct((VPAD, D), BF),
            jax.ShapeDtypeStruct((D, LEN), BF),
            jax.ShapeDtypeStruct((4, D, LEN), BF),
        ),
        in_specs=[
            pl.BlockSpec(memory_space=pltpu.SMEM),
            inside,
            inside,
            inside,
            inside,
            inside,
            anywhere,
            anywhere,
        ],
        out_specs=(anywhere, inside, inside, inside),
        scratch_shapes=[
            pltpu.VMEM((UNITS, 128, D), BF),
            pltpu.VMEM(wexpand.shape, F32),
            pltpu.VMEM(wshrink.shape, F32),
            pltpu.VMEM((4, shards, 128, D), BF),
            pltpu.VMEM((LEN // QB, 3 * QB, QB), F32),
            pltpu.VMEM((ROTARY // 2, LEN), F32),
            pltpu.VMEM((ROTARY // 2, LEN), F32),
            pltpu.VMEM((256, LEN), BF),
            pltpu.VMEM((256, LEN), BF),
            pltpu.VMEM((256, LEN), BF),
            pltpu.VMEM((256, LEN), BF),
            pltpu.VMEM((64, LEN), F32),
            pltpu.VMEM((64, LEN), F32),
            pltpu.VMEM((64, LEN), F32),
            pltpu.SemaphoreType.DMA((4, count)),
            pltpu.SemaphoreType.DMA((4, count)),
            pltpu.SemaphoreType.DMA((4, count)),
            pltpu.SemaphoreType.DMA((4, count)),
            pltpu.SemaphoreType.DMA((shards - 1,)),
            pltpu.SemaphoreType.DMA((shards - 1,)),
            pltpu.SemaphoreType.DMA((8,)),
        ],
        compiler_params=pltpu.CompilerParams(
            collective_id=0, has_side_effects=True, vmem_limit_bytes=58 * MIB
        ),
        name="front",
    )(lengths, tokens, dy, wqkv, wd, vec, wexpand, wshrink)


RC = 4


class Reduce:
    def __init__(self, at, grads, rc, rb, ra, rz, out, send, recv):
        self.at = at
        self.grads, self.rc, self.rb, self.ra, self.rz, self.out = grads, rc, rb, ra, rz, out
        self.send, self.recv = send, recv

    @staticmethod
    def sems(nz):
        return 3 + (nz - 1) + 3

    def copy(self, u, i, src, dst, peer):
        return remote(src, dst, self.send.at[u, i], self.recv.at[u, i], peer)

    def c(self, u):
        at = self.at
        return self.copy(u, 0, self.grads.at[u % 2, :, :, 1 - at.c], self.rc.at[u % RC], at.cpeer)

    def b(self, u, core):
        at = self.at
        rc = self.rc.at[u % RC]
        src = rc.at[:, :, 1 - at.y] if core == 0 else rc.at[:, 1 - at.x]
        return self.copy(u, 1, src, self.rb.at[u], at.swap(False))

    def turn(self):
        return jnp.where(self.at.c == 0, self.at.x, self.at.y)

    def a(self, u):
        src = self.rb.at[u, :, 1 - self.turn()]
        return self.copy(u, 2, src, self.ra.at[u], self.at.swap(True))

    def z(self, u, k):
        at = self.at
        src = self.ra.at[u, (at.z + k) % at.nz]
        return self.copy(u, 2 + k, src, self.rz.at[u, k - 1], at.zpeer(k))

    def f(self, u, k):
        at = self.at
        ref = self.out.at[u, at.p]
        return self.copy(u, 2 + at.nz + k, ref, ref, (at.ypeer, at.cpeer, at.diag)[k])

    def f_in(self, u, k):
        at = self.at
        c, y = (at.c if k == 0 else 1 - at.c), (at.y if k == 1 else 1 - at.y)
        ref = self.out.at[u, 2 * c + y]
        return self.copy(u, 2 + at.nz + k, ref, ref, (at.ypeer, at.cpeer, at.diag)[k])

    def phase0(self, u):
        self.c(u).start()

    def phase1(self, u):
        at = self.at
        self.c(u).wait_recv()
        add_into(self.rc.at[u % RC], self.grads.at[u % 2, :, :, at.c])
        for core in (0, 1):
            pl.when(at.c == core)(lambda core=core: self.b(u, core).start())

    def phase2(self, u):
        at = self.at
        rc = self.rc.at[u % RC]
        self.b(u, 0).wait_recv()
        pl.when(at.c == 0)(lambda: add_into(self.rb.at[u], rc.at[:, :, at.y]))
        pl.when(at.c == 1)(lambda: add_into(self.rb.at[u], rc.at[:, at.x]))
        self.a(u).start()
        self.b(u, 0).wait_send()
        self.c(u).wait_send()

    def phase3(self, u):
        self.a(u).wait_recv()
        add_into(self.ra.at[u], self.rb.at[u, :, self.turn()])
        for k in range(1, self.at.nz):
            self.z(u, k).start()

    def phase4(self, u):
        at = self.at
        total = self.ra[u, at.z].astype(F32)
        for k in range(1, at.nz):
            self.z(u, k).wait_recv()
            total += self.rz[u, k - 1].astype(F32)
        self.out[u, at.p] = total.astype(BF)
        for k in range(3):
            self.f(u, k).start()

    def phase5(self, u):
        for k in range(3):
            self.f_in(u, k).wait_recv()
            self.f(u, k).wait_send()
        self.a(u).wait_send()
        for k in range(1, self.at.nz):
            self.z(u, k).wait_send()


PHASES = 6


def add_into(dst, src):
    dst[...] = (dst[...].astype(F32) + src[...].astype(F32)).astype(BF)


class VecSum:
    def __init__(self, shards, reps, gvec, v1, v2, sq, send, recv):
        self.shards, self.reps = shards, reps
        self.r, self.s = lax.axis_index("rep"), lax.axis_index("shard")
        self.row = [{"rep": self.r, "shard": (self.s + k) % shards} for k in range(1, shards)]
        self.col = [{"rep": (self.r + k) % reps, "shard": self.s} for k in range(1, reps)]
        self.gvec, self.v1, self.v2, self.sq = gvec, v1, v2, sq
        self.send, self.recv = send, recv

    @staticmethod
    def sems(shards, reps):
        return 2 * (shards - 1) + reps - 1

    def lanes(self, i):
        return pl.ds(pl.multiple_of(i * 128, 128), 128)

    def copy(self, i, src, dst, peer):
        return remote(src, dst, self.send.at[i], self.recv.at[i], peer)

    def over_shards(self, k):
        src = self.gvec.at[:, self.lanes((self.s + k) % self.shards)]
        return self.copy(k - 1, src, self.v1.at[self.s], self.row[k - 1])

    def over_reps(self, k):
        ref = self.v2.at[self.r]
        return self.copy(self.shards + k - 2, ref, ref, self.col[k - 1])

    def squares(self, k):
        ref = self.sq.at[self.s]
        return self.copy(self.shards + self.reps + k - 3, ref, ref, self.row[k - 1])

    def total(self, ref, count):
        every = ref[0]
        for i in range(1, count):
            every += ref[i]
        return every

    def stage0(self):
        for k in range(1, self.shards):
            self.over_shards(k).start()
        self.v1[self.s] = self.gvec[:, self.lanes(self.s)]

    def stage1(self):
        for k in range(1, self.shards):
            dst = self.v1.at[(self.s + self.shards - k) % self.shards]
            self.copy(k - 1, dst, dst, self.row[k - 1]).wait_recv()
            self.over_shards(k).wait_send()
        self.v2[self.r] = self.total(self.v1, self.shards)
        for k in range(1, self.reps):
            self.over_reps(k).start()

    def stage2(self):
        for k in range(1, self.reps):
            dst = self.v2.at[(self.r + self.reps - k) % self.reps]
            self.copy(self.shards + k - 2, dst, dst, self.col[k - 1]).wait_recv()
            self.over_reps(k).wait_send()
        return self.total(self.v2, self.reps)

    def norm(self, wide, table):
        part = table[:8] * table[:8] + table[8:] * table[8:]
        for i in range(D // 128):
            part += wide[:, i * 128 : i * 128 + 128]
        self.sq[self.s] = part
        for k in range(1, self.shards):
            self.squares(k).start()
        for k in range(1, self.shards):
            i = self.shards + self.reps + k - 3
            dst = self.sq.at[(self.s + self.shards - k) % self.shards]
            self.copy(i, dst, dst, self.row[k - 1]).wait_recv()
            self.squares(k).wait_send()
        return jnp.sqrt(jnp.sum(self.total(self.sq, self.shards), keepdims=True))


def fold_squares(block):
    g = block.astype(F32)
    return jnp.sum((g * g).reshape(-1, 8, D), axis=0)


def cols(n):
    return pl.ds(pl.multiple_of(n * 256, 256), 256)


def tiles(run):
    def one(n, carry):
        run(n)
        return carry

    lax.fori_loop(0, D // 256, one, 0)


def back_kernel(
    nz, reps,
    tokens, dy, ht, table, act, full,
    out, grad_in, owned, gtable, norm,
    wb, grads, rc, rb, ra, rz, gelu, dact, acc, b1, gb1, gv, wide, v1, v2, sq,
    send, recv, vsend, vrecv, wsem,
):
    at = Place(nz)
    shards = 2 * nz
    fused = reps == 4
    width = FF // shards
    load_first = lambda q, src: pltpu.make_async_copy(src, wb.at[q % 2, 0], wsem.at[q % 2, 0])
    load_second = lambda q, src: pltpu.make_async_copy(src, wb.at[q % 2, 1], wsem.at[q % 2, 1])

    load_first(0, act.at[0]).start()
    load_second(0, full.at[0]).start()
    red = Reduce(at, grads, rc, rb, ra, rz, owned, send, recv)
    vecs = VecSum(shards, reps, gv, v1, v2, sq, vsend, vrecv)
    gv[...] = jnp.zeros((VPAD, D), F32)
    wide[...] = jnp.zeros((8, D), F32)
    for j in range(FF // D):
        for s in range(shards):
            f = s * width + j * 128
            b1[j : j + 1, s * 128 : s * 128 + 128] = table[
                6 + f // D : 7 + f // D, f % D : f % D + 128
            ].astype(F32)
    greet(vecs.row + [at.ypeer, at.cpeer, at.diag])

    def write(u, n, value):
        grads[u % 2, :, :, :, :, :, cols(n)] = value.astype(BF).reshape(nz, 2, 2, 2, 32, 256)

    def activate(slot, j):
        def tile(n):
            a = dot(ht[...], wb[slot, 1, :, cols(n)], 0, 0) + b1[pl.ds(j, 1), cols(n)]
            square = a * a
            t = jnp.tanh(math.sqrt(2.0 / math.pi) * a * (1.0 + 0.044715 * square))
            half = 0.5 * (1.0 + t)
            gelu[:, cols(n)] = (a * half).astype(BF)
            slope = half + 0.5 * a * (1.0 - t * t) * (
                math.sqrt(2.0 / math.pi) * (1.0 + 3 * 0.044715 * square)
            )
            da = (dot(dy[...], wb[slot, 0, cols(n), :], 1, 1) * slope).astype(BF)
            dact[:, cols(n)] = da
            gb1[pl.ds(j, 1), cols(n)] = jnp.sum(da.astype(F32), axis=0, keepdims=True)

        tiles(tile)

    def finish():
        gain = table[0:1].astype(F32)
        shift = table[5:6].astype(F32) + table[10:11].astype(F32)

        def rows_of(i, carry):
            rows = pl.ds(pl.multiple_of(i * 128, 128), 128)
            x = tokens[rows].astype(F32)
            out[rows] = (x + acc[rows] + shift).astype(BF)
            centered = x - jnp.mean(x, axis=1, keepdims=True)
            rstd = lax.rsqrt(jnp.mean(centered * centered, axis=1, keepdims=True) + 1e-05)
            n = centered * rstd
            dh = grad_in[rows]
            back = dy[rows].astype(F32)
            e = dh * gain
            grad_in[rows] = back + rstd * (
                e
                - jnp.mean(e, axis=1, keepdims=True)
                - n * jnp.mean(e * n, axis=1, keepdims=True)
            )
            gv[0:1] += jnp.sum(dh * n, axis=0, keepdims=True)
            gv[1:2] += jnp.sum(dh, axis=0, keepdims=True)
            gv[5:6] += jnp.sum(back, axis=0, keepdims=True)
            return carry

        lax.fori_loop(0, LEN // 128, rows_of, 0)
        gv[10:11] = gv[5:6]
        for j in range(FF // D):
            for s in range(shards):
                f = s * width + j * 128
                gv[6 + f // D : 7 + f // D, f % D : f % D + 128] = gb1[
                    j : j + 1, s * 128 : s * 128 + 128
                ]

    def tick(t, carry):
        for number in range(1, PHASES):
            u = t - number

            def phase(u=u, number=number):
                getattr(red, f"phase{number}")(u)
                if number == 5 and fused:
                    wide[...] += fold_squares(owned[u])

            pl.when((u >= 0) & (u < UNITS))(phase)

        q = jnp.where(t < 4, t, 4 + (t - 4) // 2)
        slot = q % 2
        j = q - 4

        @pl.when((t < UNITS) & ((t < 4) | (t % 2 == 0)))
        def _():
            load_first(q, full.at[0]).wait()
            load_second(q, full.at[0]).wait()

            @pl.when(q + 1 < 4)
            def _():
                load_first(q + 1, act.at[q + 1]).start()
                load_second(q + 1, full.at[q + 1]).start()

            @pl.when((q + 1 >= 4) & (q + 1 < 8))
            def _():
                load_first(q + 1, full.at[2 * (q + 1) - 4]).start()
                load_second(q + 1, full.at[2 * (q + 1) - 3]).start()

        dense, qkv = t == 0, (t >= 1) & (t < 4)
        mlp = (t >= 4) & (t < UNITS)
        shrink, expand = mlp & (t % 2 == 0), mlp & (t % 2 == 1)

        pl.when(shrink)(lambda: activate(slot, j))
        pl.when(dense)(
            lambda: tiles(lambda n: write(t, n, dot(wb[slot, 0], dy[:, cols(n)], 1, 0)))
        )
        pl.when(qkv)(
            lambda: tiles(lambda n: write(t, n, dot(ht[...], wb[slot, 0, cols(n), :], 1, 1)))
        )
        pl.when(shrink)(
            lambda: tiles(lambda n: write(t, n, dot(gelu[...], dy[:, cols(n)], 0, 0)))
        )
        pl.when(expand)(
            lambda: tiles(lambda n: write(t, n, dot(ht[...], dact[:, cols(n)], 1, 0)))
        )
        pl.when(t < UNITS)(lambda: red.phase0(t))

        @pl.when(dense)
        def _():
            def tile(n):
                acc[:, cols(n)] = dot(wb[slot, 0], wb[slot, 1, :, cols(n)], 0, 0)
                grad_in[:, cols(n)] = jnp.zeros((LEN, 256), F32)

            tiles(tile)

        @pl.when(qkv)
        def _():
            ones = jnp.ones((8, LEN), BF)

            def tile(n):
                grad_in[:, cols(n)] += dot(wb[slot, 0], wb[slot, 1, cols(n), :], 0, 1)
                gv[pl.ds(t + 1, 1), cols(n)] = dot(ones, wb[slot, 0, cols(n), :], 1, 1)[:1]

            tiles(tile)

        @pl.when(expand)
        def _():
            def tile(n):
                acc[:, cols(n)] += dot(gelu[...], wb[slot, 0, :, cols(n)], 1, 0)
                grad_in[:, cols(n)] += dot(dact[...], wb[slot, 1, cols(n), :], 1, 1)

            tiles(tile)

        pl.when(t == UNITS)(finish)
        if fused:
            pl.when(t == UNITS)(vecs.stage0)
            pl.when(t == UNITS + 1)(vecs.stage1)

            @pl.when(t == UNITS + 2)
            def _():
                gtable[...] = vecs.stage2()

        return carry

    lax.fori_loop(0, UNITS + PHASES - 1, tick, 0)
    if fused:
        norm[...] = vecs.norm(wide[...], gtable[...])
    else:
        gtable[...] = gv[...]
        norm[...] = jnp.zeros((1, 1), F32)


def back(tokens, dy, ht, table, act, full, nz, reps):
    shards = 2 * nz
    count = Reduce.sems(nz)
    vcount = VecSum.sems(shards, reps)
    anywhere = pl.BlockSpec(memory_space=pl.ANY)
    inside = pl.BlockSpec(memory_space=pltpu.VMEM)

    def kernel(*refs):
        back_kernel(nz, reps, *refs)

    return pl.pallas_call(
        kernel,
        out_shape=(
            jax.ShapeDtypeStruct((LEN, D), BF),
            jax.ShapeDtypeStruct((LEN, D), F32),
            jax.ShapeDtypeStruct((UNITS, 4, 32, D), BF),
            jax.ShapeDtypeStruct((VPAD, 128 if reps == 4 else D), F32),
            jax.ShapeDtypeStruct((1, 1), F32),
        ),
        in_specs=[inside, inside, inside, inside, anywhere, anywhere],
        out_specs=(inside,) * 5,
        scratch_shapes=[
            pltpu.VMEM((2, 2, D, D), BF),
            pltpu.VMEM((2, nz, 2, 2, 2, 32, D), BF),
            pltpu.VMEM((RC, nz, 2, 2, 32, D), BF),
            pltpu.VMEM((UNITS, nz, 2, 32, D), BF),
            pltpu.VMEM((UNITS, nz, 32, D), BF),
            pltpu.VMEM((UNITS, nz - 1, 32, D), BF),
            pltpu.VMEM((LEN, D), BF),
            pltpu.VMEM((LEN, D), BF),
            pltpu.VMEM((LEN, D), F32),
            pltpu.VMEM((FF // D, D), F32),
            pltpu.VMEM((FF // D, D), F32),
            pltpu.VMEM((VPAD, D), F32),
            pltpu.VMEM((8, D), F32),
            pltpu.VMEM((shards, VPAD, 128), F32),
            pltpu.VMEM((reps, VPAD, 128), F32),
            pltpu.VMEM((shards, 8, 128), F32),
            pltpu.SemaphoreType.DMA((UNITS, count)),
            pltpu.SemaphoreType.DMA((UNITS, count)),
            pltpu.SemaphoreType.DMA((vcount,)),
            pltpu.SemaphoreType.DMA((vcount,)),
            pltpu.SemaphoreType.DMA((2, 2)),
        ],
        compiler_params=pltpu.CompilerParams(
            collective_id=1, has_side_effects=True, vmem_limit_bytes=60 * MIB
        ),
        name="back",
    )(tokens, dy, ht, table, act, full)


def norm_kernel(shards, reps, gvec, own, gtable, norm, v1, v2, sq, send, recv):
    vecs = VecSum(shards, reps, gvec, v1, v2, sq, send, recv)
    greet(vecs.row + vecs.col)
    vecs.stage0()
    wide = lax.fori_loop(
        0, own.shape[0], lambda u, acc: acc + fold_squares(own[u]), jnp.zeros((8, D), F32)
    )
    vecs.stage1()
    gtable[...] = vecs.stage2()
    norm[...] = vecs.norm(wide, gtable[...])


def norm_all(gvec, own, shards, reps):
    count = VecSum.sems(shards, reps)

    def kernel(*refs):
        norm_kernel(shards, reps, *refs)

    inside = pl.BlockSpec(memory_space=pltpu.VMEM)
    return pl.pallas_call(
        kernel,
        out_shape=(
            jax.ShapeDtypeStruct((VPAD, 128), F32),
            jax.ShapeDtypeStruct((1, 1), F32),
        ),
        in_specs=[inside, inside],
        out_specs=(inside, inside),
        scratch_shapes=[
            pltpu.VMEM((shards, VPAD, 128), F32),
            pltpu.VMEM((reps, VPAD, 128), F32),
            pltpu.VMEM((shards, 8, 128), F32),
            pltpu.SemaphoreType.DMA((count,)),
            pltpu.SemaphoreType.DMA((count,)),
        ],
        compiler_params=pltpu.CompilerParams(
            collective_id=2, has_side_effects=True, vmem_limit_bytes=56 * MIB
        ),
        name="norm_all",
    )(gvec, own)


def adamw(master, firsts, seconds, gradient, factor, step_rate, decay_amount):
    clipped = gradient * factor
    momentum = 0.9 * firsts + 0.1 * clipped
    variance = 0.95 * seconds + 0.05 * clipped * clipped
    corrected = momentum / (1.0 - 0.9**STEP)
    spread = variance / (1.0 - 0.95**STEP)
    renewed = master - step_rate * (corrected / (jnp.sqrt(spread) + 1e-08) + decay_amount * master)
    return (momentum, variance, renewed)


def update_kernel(shards, norm, own, own_shrink, *refs):
    ins, outs = refs[:12], refs[12:]
    factor = jnp.minimum(1.0, clip_limit / (norm[...] + 1e-06))
    width = FF // shards

    def part(number, rows, lanes, gradient):
        trio = ins[3 * number : 3 * number + 3]
        new = adamw(
            *(ref[rows, lanes] for ref in trio), gradient.astype(F32), factor, matrix_rate, decay_rate
        )
        for ref, value in zip(outs[3 * number : 3 * number + 3], new):
            ref[rows, lanes] = value

    every = slice(None)
    for i in range(3):
        part(0, every, slice(i * D, i * D + D), own[1 + i])
    part(1, every, every, own[0])
    for j in range(FF // D):
        for s in range(shards):
            f = s * width + j * 128
            part(2, every, slice(f, f + 128), own[5 + 2 * j, :, s * 128 : s * 128 + 128])
    part(3, every, every, own_shrink[0])


def update_all(norm, own, states, shards):
    steps = 8
    rows = 128 // steps
    specs = []
    for master in states[::3]:
        height, lanes = master.shape
        specs += [pl.BlockSpec((height // steps, lanes), lambda i: (i, 0))] * 3

    def kernel(*refs):
        update_kernel(shards, *refs)

    return pl.pallas_call(
        kernel,
        grid=(steps,),
        out_shape=tuple(jax.ShapeDtypeStruct(a.shape, F32) for a in states),
        in_specs=[
            pl.BlockSpec((1, 1), lambda i: (0, 0)),
            pl.BlockSpec((UNITS, rows, D), lambda i: (0, i, 0)),
            pl.BlockSpec((1, 4 * rows, D), lambda i: (4 + 2 * (i // 2), i % 2, 0)),
        ]
        + specs,
        out_specs=tuple(specs),
        compiler_params=pltpu.CompilerParams(vmem_limit_bytes=56 * MIB),
        name="update",
    )(norm, own, own, *states)


def body(
    tokens,
    doc_lengths,
    cotangent,
    qkv_weight,
    qkv_firsts,
    qkv_seconds,
    dense_weight,
    dense_firsts,
    dense_seconds,
    expand_weight,
    expand_firsts,
    expand_seconds,
    shrink_weight,
    shrink_firsts,
    shrink_seconds,
    vectors,
    vec_firsts,
    vec_seconds,
    *,
    shards,
    reps,
):
    nz = shards // 2
    vec_own = jnp.pad(vectors.astype(BF).T, ((0, VPAD - VROWS), (0, 0)))
    full, table, ht, act = front(
        doc_lengths, tokens, cotangent, qkv_weight, dense_weight, vec_own, expand_weight, shrink_weight, nz
    )
    output, grad_in, owned, gtable, norm = back(
        tokens, cotangent, ht, table, act, full.reshape(UNITS, D, D), nz, reps
    )
    owned = owned.reshape(UNITS, 128, D)
    if reps != 4:
        quads = [[4 * i + j for i in range(reps // 4)] for j in range(4)]
        owned = lax.psum(owned, "rep", axis_index_groups=quads)
        gtable, norm = norm_all(gtable, owned, shards, reps)
    states = (
        qkv_weight, qkv_firsts, qkv_seconds,
        dense_weight, dense_firsts, dense_seconds,
        expand_weight, expand_firsts, expand_seconds,
        shrink_weight, shrink_firsts, shrink_seconds,
    )
    updates = []
    new = update_all(norm, owned, states, shards)
    for i in range(4):
        renewed, momentum, variance = 3 * i + 2, 3 * i, 3 * i + 1
        updates += [new[momentum], new[variance], new[renewed]]
    grad_norm = norm.reshape(1)
    factor = jnp.minimum(1.0, clip_limit / (grad_norm + 1e-06))
    updates += adamw(
        vectors, vec_firsts, vec_seconds, gtable[:VROWS].T, factor, vector_rate, 0.0
    )
    return (output, grad_in) + tuple(updates) + (grad_norm,)


def solution(mesh):
    shards, reps = mesh.shape["shard"], mesh.shape["rep"]
    data, state = P(("rep", "shard"), None), P("shard", None)

    def step(*args):
        return body(*args, shards=shards, reps=reps)

    return jax.shard_map(
        step,
        mesh=mesh,
        in_specs=(data, data, data) + (state,) * 15,
        out_specs=(data, data) + (state,) * 15 + (P(),),
        check_vma=False,
    )
```

```python
import math

import jax
import jax.numpy as jnp
from jax import lax
from jax.experimental import pallas as pl
from jax.experimental.pallas import tpu as pltpu
from jax.sharding import PartitionSpec as P

D = 1024
HEADS = 16
HEAD_DIM = 64
ROTARY = 32
FF = 4096
LEN = 1024
STEP = 10
VROWS = 11
VPAD = 16
UNITS = 12
QB = 256

clip_limit = 1.0
matrix_rate = 0.05
vector_rate = 0.8
decay_rate = 0.1

BF = jnp.bfloat16
F32 = jnp.float32
MIB = 1 << 20


def dot(a, b, ca, cb):
    return lax.dot_general(a, b, (((ca,), (cb,)), ((), ())), preferred_element_type=F32)


class Place:
    def __init__(self, nz):
        self.nz = nz
        self.r = lax.axis_index("rep")
        self.s = lax.axis_index("shard")
        self.z, self.x = self.s // 2, self.s % 2
        self.c = self.r % 2
        self.y = (self.r // 2) % 2
        self.p = 2 * self.c + self.y

    def dev(self, r, s):
        return {"rep": r, "shard": s}

    def zpeer(self, k):
        return self.dev(self.r, ((self.z + k) % self.nz) * 2 + self.x)

    @property
    def xpeer(self):
        return self.dev(self.r, self.z * 2 + 1 - self.x)

    @property
    def ypeer(self):
        return self.dev(self.r + 2 - 4 * self.y, self.s)

    @property
    def cpeer(self):
        return self.dev(self.r + 1 - 2 * self.c, self.s)

    @property
    def diag(self):
        return self.dev(self.r + 2 - 4 * self.y + 1 - 2 * self.c, self.s)

    def swap(self, first):
        on_x = self.c == (0 if first else 1)
        return self.dev(
            jnp.where(on_x, self.r, self.r + 2 - 4 * self.y),
            jnp.where(on_x, self.z * 2 + 1 - self.x, self.s),
        )


def greet(peers):
    barrier = pltpu.get_barrier_semaphore()
    for peer in peers:
        pl.semaphore_signal(barrier, inc=1, device_id=peer, device_id_type=pl.DeviceIdType.MESH)
    pl.semaphore_wait(barrier, len(peers))


def remote(src, dst, send, recv, peer):
    return pltpu.make_async_remote_copy(
        src_ref=src,
        dst_ref=dst,
        send_sem=send,
        recv_sem=recv,
        device_id=peer,
        device_id_type=pl.DeviceIdType.MESH,
    )


class Gather:
    STAGES = 5

    def __init__(self, at, own, full, u0, n, lane, width, send, recv, job):
        self.at, self.own, self.full = at, own, full
        self.us, self.lanes = pl.ds(u0, n), pl.ds(lane, width)
        self.send, self.recv, self.job = send, recv, job

    def rows(self, count):
        at = self.at
        return pl.ds(at.c * 64 + at.y * 32, 32) if count == 32 else pl.ds(at.c * 64, 64)

    def part(self, z, x, rows):
        return self.full.at[self.us, z, x, rows, self.lanes]

    def copy(self, i, src, dst, peer):
        return remote(src, dst, self.send.at[self.job, i], self.recv.at[self.job, i], peer)

    def all_of(self, i):
        every = slice(None)
        z, x, count = ((pl.ds(0, self.at.nz - 1), 0, 32), (every, 0, 32), (every, every, 32), (every, every, 64))[i]
        ref = self.part(z, x, pl.ds(0, count))
        return self.copy(i, ref, ref, self.at.cpeer)

    def stage0(self):
        at = self.at
        src = self.own.at[self.us, self.rows(32), self.lanes]
        for k in range(1, at.nz):
            self.copy(0, src, self.part(at.z, at.x, self.rows(32)), at.zpeer(k)).start()

    def stage1(self):
        self.all_of(0).wait_recv()
        ref = self.part(slice(None), self.at.x, self.rows(32))
        self.copy(1, ref, ref, self.at.swap(True)).start()

    def stage2(self):
        at = self.at
        self.all_of(1).wait_recv()
        along_y = self.part(slice(None), slice(None), self.rows(32))
        along_x = self.part(slice(None), at.x, self.rows(64))
        pl.when(at.c == 0)(lambda: self.copy(2, along_y, along_y, at.ypeer).start())
        pl.when(at.c == 1)(lambda: self.copy(2, along_x, along_x, at.xpeer).start())

    def stage3(self):
        self.all_of(2).wait_recv()
        ref = self.part(slice(None), slice(None), self.rows(64))
        self.copy(3, ref, ref, self.at.cpeer).start()

    def stage4(self):
        self.all_of(3).wait_recv()
        for i in range(4):
            self.all_of(i).wait_send()


def rotate_rows(u, cosine, sine):
    top = u[:16] * cosine - u[16:32] * sine
    low = u[16:32] * cosine + u[:16] * sine
    return jnp.concatenate([top, low, u[32:]], axis=0)


def heads_attention(base, bias, qt, kt, vt, gt, act, dqt, dkt, dvt, pause):
    def scores(head, number):
        q0 = number * QB
        k0 = max(0, number - 2) * QB
        span = q0 + QB - k0
        rows = slice(64 * head, 64 * head + 64)
        q, g = qt[rows, q0 : q0 + QB], gt[rows, q0 : q0 + QB]
        k, v = kt[rows, k0 : k0 + span], vt[rows, k0 : k0 + span]
        return q, g, k, v, dot(k, q, 0, 0) + bias[number, :span], dot(v, g, 0, 0)

    def weigh(head, number, q, g, k, v, s, dp):
        outs = pl.ds(pl.multiple_of(base + 64 * head, 64), 64)
        e = jnp.exp(s - jnp.max(s, axis=0, keepdims=True))
        p = e * (1.0 / jnp.sum(e, axis=0, keepdims=True))
        pb = p.astype(BF)
        o = dot(v, pb, 1, 0)
        inner = jnp.sum(o * g.astype(F32), axis=0, keepdims=True)
        ds = (p * (dp - inner)).astype(BF)
        act[0, outs, number * QB : number * QB + QB] = o.astype(BF)
        return q, g, k, pb, ds

    def spread(head, number, q, g, k, pb, ds):
        q0 = number * QB
        k0 = max(0, number - 2) * QB
        old = q0 - k0
        rows = slice(64 * head, 64 * head + 64)
        dqt[rows, q0 : q0 + QB] = dot(k, ds, 1, 0)
        dk = dot(q, ds, 1, 1)
        dv = dot(g, pb, 1, 1)
        if old:
            dkt[rows, k0:q0] += dk[:, :old]
            dvt[rows, k0:q0] += dv[:, :old]
        dkt[rows, q0 : q0 + QB] = dk[:, old:]
        dvt[rows, q0 : q0 + QB] = dv[:, old:]

    order = [(head, number) for number in range(LEN // QB) for head in range(4)]
    ready, waiting = scores(*order[0]), None
    for i, (head, number) in enumerate(order):
        following = scores(*order[i + 1]) if i + 1 < len(order) else None
        weighed = weigh(head, number, *ready)
        if waiting is not None:
            spread(*waiting)
        waiting, ready = (head, number, *weighed), following
        if i % 4 == 3:
            pause(i // 4)
    spread(*waiting)


JOBS = UNITS + 1
READY = 6
LAGS = (0, 2, 3, 5, 6)


def run_stage(gather, stage):
    getattr(gather, f"stage{stage}")()


def front_kernel(
    nz,
    lengths, tokens, dy, wqkv, wd, vec, wexpand, wshrink,
    full, table, ht, act,
    own, expand_f, shrink_f, wd_v, wq_v, bias, cosine, sine, qt, kt, vt, gt, dqf, dkf, dvf,
    send, recv, vsend, vrecv, lsem,
):
    at = Place(nz)
    shards = 2 * nz
    others = [at.dev(at.r, (at.s + k) % shards) for k in range(1, shards)]
    load_expand = pltpu.make_async_copy(wexpand, expand_f, lsem.at[0])
    load_shrink = pltpu.make_async_copy(wshrink, shrink_f, lsem.at[1])
    load_expand.start()
    load_shrink.start()
    own[0] = wd[...].astype(BF)
    for i in range(3):
        own[1 + i] = wqkv[:, i * D : i * D + D].astype(BF)
    greet(others + [at.ypeer, at.cpeer])

    def lanes(i):
        return pl.ds(pl.multiple_of(i * 128, 128), 128)

    vcopies = [
        remote(vec, table.at[:, lanes(at.s)], vsend.at[k], vrecv.at[k], peer)
        for k, peer in enumerate(others)
    ]
    for copy in vcopies:
        copy.start()
    table[:, lanes(at.s)] = vec[...]
    mine = pl.ds(at.p * 32, 32)
    local_a = pltpu.make_async_copy(
        own.at[0:4, mine], full.at[0:4, at.z, at.x, mine], lsem.at[2]
    )
    local_a.start()
    local_f = pltpu.make_async_copy(
        own.at[4:UNITS, mine], full.at[4:UNITS, at.z, at.x, mine], lsem.at[3]
    )

    def cast_rest():
        load_expand.wait()
        load_shrink.wait()
        width = FF // shards
        for j in range(FF // D):
            own[4 + 2 * j] = shrink_f[j * 128 : j * 128 + 128].astype(BF)
            for b in range(shards):
                own[5 + 2 * j, :, b * 128 : b * 128 + 128] = expand_f[
                    :, b * width + j * 128 : b * width + j * 128 + 128
                ].astype(BF)
        local_f.start()

    def tables():
        place = lax.broadcasted_iota(jnp.int32, (1, LEN), 1)
        start = jnp.zeros((1, LEN), jnp.int32)
        end = 0
        for d in range(lengths.shape[1]):
            end = end + lengths[0, d]
            start = start + jnp.where(place >= end, lengths[0, d], 0)
        m = lax.broadcasted_iota(jnp.int32, (ROTARY // 2, LEN), 0).astype(F32)
        frequency = jnp.exp(m * (-2.0 * math.log(10000.0) / ROTARY))
        angle = (place - start).astype(F32) * frequency
        cosine[...] = jnp.cos(angle)
        sine[...] = jnp.sin(angle)
        for number in range(LEN // QB):
            q0 = number * QB
            k0 = max(0, number - 2) * QB
            span = q0 + QB - k0
            j = k0 + lax.broadcasted_iota(jnp.int32, (span, QB), 0)
            i = q0 + lax.broadcasted_iota(jnp.int32, (span, QB), 1)
            allowed = (j >= start[:, q0 : q0 + QB]) & (j <= i)
            bias[number, :span] = jnp.where(allowed, 0.0, -1e30)

    def wait_vec():
        for k, copy in enumerate(vcopies):
            came = (at.s + shards - (k + 1)) % shards
            remote(vec, table.at[:, lanes(came)], vsend.at[k], vrecv.at[k], others[k]).wait_recv()
            copy.wait_send()

    def norm_rows(i):
        rows = pl.ds(pl.multiple_of(i * 256, 256), 256)
        x = tokens[rows].astype(F32)
        centered = x - jnp.mean(x, axis=1, keepdims=True)
        scaled = centered * lax.rsqrt(jnp.mean(centered * centered, axis=1, keepdims=True) + 1e-05)
        h = scaled * table[0:1].astype(F32) + table[1:2].astype(F32)
        ht[:, rows] = h.astype(BF).T

    def part(job, stage):
        args = (send, recv, job)
        if isinstance(job, int):
            if job == 1:
                gather = Gather(at, own, full, 0, 1, 0, D, *args)
            elif job < 5:
                gather = Gather(at, own, full, 1, 3, 256 * max(0, job - 1), 256, *args)
            else:
                gather = Gather(at, own, full, job - 1, 1, 0, D, *args)
            run_stage(gather, stage)
            return
        lane = pl.multiple_of((job - 1) * 256, 256)
        pl.when((job >= 2) & (job < 5))(
            lambda: run_stage(Gather(at, own, full, 1, 3, lane, 256, *args), stage)
        )
        pl.when((job >= 5) & (job < JOBS))(
            lambda: run_stage(Gather(at, own, full, job - 1, 1, 0, D, *args), stage)
        )

    def load_quad(quad):
        lane = quad * 256 if isinstance(quad, int) else pl.multiple_of(quad * 256, 256)
        src = full.at[pl.ds(1, 3), :, :, :, pl.ds(lane, 256)]
        return pltpu.make_async_copy(src, wq_v.at[quad % 2], lsem.at[4 + quad % 2])

    load_dense = pltpu.make_async_copy(full.at[0], wd_v, lsem.at[6])
    side = {
        0: (tables,),
        1: (wait_vec, lambda: norm_rows(0)),
        2: (lambda: norm_rows(1), lambda: norm_rows(2)),
        3: (lambda: norm_rows(3),),
        4: (cast_rest,),
    }
    for step in range(READY):
        for stage in range(Gather.STAGES):
            if 0 <= step - stage < 2:
                if step == 1 and stage == 1:
                    local_a.wait()
                part(step - stage, stage)
            if step - LAGS[stage] >= 2:
                part(step - LAGS[stage], stage)
        for what in side.get(step, ()):
            what()
        if step == 4:
            load_quad(0).start()
    load_dense.start()
    local_f.wait()

    def prepare(quad):
        cols = pl.ds(pl.multiple_of(quad * 256, 256), 256)
        load_quad(quad).wait()
        pl.when(quad == 0)(load_dense.wait)
        for part, dst in enumerate((qt, kt, vt)):
            w = wq_v[quad % 2, part].reshape(D, 256)
            u = dot(w, ht[...], 0, 0)
            ones = jnp.ones((1, 128), BF)
            b = dot(table[2 + part : 3 + part, cols], ones, 0, 0)[:, :1]
            u = u + b
            if part == 2:
                dst[...] = u.astype(BF)
                continue
            for head in range(4):
                turned = rotate_rows(u[head * 64 : head * 64 + 64], cosine[...], sine[...])
                if part == 0:
                    turned = turned * (1.0 / math.sqrt(HEAD_DIM))
                dst[head * 64 : head * 64 + 64] = turned.astype(BF)
        for half in range(2):
            w = wd_v[quad, half]
            gt[half * 128 : half * 128 + 128] = dot(w, dy[...], 1, 1).astype(BF)

    def one_quad(quad, carry):
        prepare(quad)
        base = quad * 256

        def pause(number):
            i, left = quad * 4 + number, JOBS + LAGS[-1] - READY
            before, after = ((n * left + HEADS - 1) // HEADS for n in (i, i + 1))

            @pl.when(after > before)
            def _():
                for stage, lag in enumerate(LAGS):
                    part(READY + before - lag, stage)

            if number == 2:
                pl.when(quad < 3)(lambda: load_quad(quad + 1).start())

        heads_attention(base, bias, qt, kt, vt, gt, act, dqf, dkf, dvf, pause)
        for head in range(4):
            rows = slice(64 * head, 64 * head + 64)
            outs = pl.ds(pl.multiple_of(base + 64 * head, 64), 64)
            back = rotate_rows(dqf[rows], cosine[...], -sine[...]) * (1.0 / math.sqrt(HEAD_DIM))
            act[1, outs] = back.astype(BF)
            act[2, outs] = rotate_rows(dkf[rows], cosine[...], -sine[...]).astype(BF)
            act[3, outs] = dvf[rows].astype(BF)
        return carry

    lax.fori_loop(0, 4, one_quad, 0)


def front(lengths, tokens, dy, wqkv, wd, vec, wexpand, wshrink, nz):
    shards = 2 * nz
    anywhere = pl.BlockSpec(memory_space=pl.ANY)
    inside = pl.BlockSpec(memory_space=pltpu.VMEM)

    def kernel(*refs):
        front_kernel(nz, *refs)

    return pl.pallas_call(
        kernel,
        out_shape=(
            jax.ShapeDtypeStruct((UNITS, nz, 2, 128, D), BF),
            jax.ShapeDtypeStruct((VPAD, D), BF),
            jax.ShapeDtypeStruct((D, LEN), BF),
            jax.ShapeDtypeStruct((4, D, LEN), BF),
        ),
        in_specs=[
            pl.BlockSpec(memory_space=pltpu.SMEM),
            inside,
            inside,
            inside,
            inside,
            inside,
            anywhere,
            anywhere,
        ],
        out_specs=(anywhere, inside, inside, inside),
        scratch_shapes=[
            pltpu.VMEM((UNITS, 128, D), BF),
            pltpu.VMEM(wexpand.shape, F32),
            pltpu.VMEM(wshrink.shape, F32),
            pltpu.VMEM((nz, 2, 128, D), BF),
            pltpu.VMEM((2, 3, nz, 2, 128, 256), BF),
            pltpu.VMEM((LEN // QB, 3 * QB, QB), F32),
            pltpu.VMEM((ROTARY // 2, LEN), F32),
            pltpu.VMEM((ROTARY // 2, LEN), F32),
            pltpu.VMEM((256, LEN), BF),
            pltpu.VMEM((256, LEN), BF),
            pltpu.VMEM((256, LEN), BF),
            pltpu.VMEM((256, LEN), BF),
            pltpu.VMEM((256, LEN), F32),
            pltpu.VMEM((256, LEN), F32),
            pltpu.VMEM((256, LEN), F32),
            pltpu.SemaphoreType.DMA((JOBS, 4)),
            pltpu.SemaphoreType.DMA((JOBS, 4)),
            pltpu.SemaphoreType.DMA((shards - 1,)),
            pltpu.SemaphoreType.DMA((shards - 1,)),
            pltpu.SemaphoreType.DMA((8,)),
        ],
        compiler_params=pltpu.CompilerParams(
            collective_id=0, has_side_effects=True, vmem_limit_bytes=58 * MIB
        ),
        name="front",
    )(lengths, tokens, dy, wqkv, wd, vec, wexpand, wshrink)


RC, RB = 3, 6


class Reduce:
    def __init__(self, at, grads, rc, rb, ra, rz, out, send, recv):
        self.at = at
        self.grads, self.rc, self.rb, self.ra, self.rz, self.out = grads, rc, rb, ra, rz, out
        self.send, self.recv = send, recv

    SEMS = 6

    def copy(self, u, i, src, dst, peer):
        send = self.send.at[u, i] if i < 3 else self.send.at[UNITS, i]
        return remote(src, dst, send, self.recv.at[u, i], peer)

    def finish(self):
        pieces = self.out.at[:, pl.ds(0, 1)], self.out.at[:, pl.ds(0, 2)]
        for i, ref in enumerate((self.rz,) + pieces):
            remote(ref, ref, self.send.at[UNITS, 3 + i], self.recv.at[0, 3 + i], self.at.cpeer).wait_send()

    def c(self, u):
        at = self.at
        return self.copy(u, 0, self.grads.at[u % 2, :, :, 1 - at.c], self.rc.at[u % RC], at.cpeer)

    def on_x(self, u):
        return (self.at.c == 1) | (u % 4 == 3)

    def b(self, u, on_x):
        at = self.at
        rc = self.rc.at[u % RC]
        src = rc.at[:, 1 - at.x] if on_x else rc.at[:, :, 1 - at.y]
        return self.copy(u, 1, src, self.rb.at[u % RB], at.xpeer if on_x else at.ypeer)

    def a(self, u, on_x):
        at = self.at
        src = self.rb.at[u % RB, :, 1 - (at.y if on_x else at.x)]
        return self.copy(u, 2, src, self.ra.at[u], at.ypeer if on_x else at.xpeer)

    def z(self, u, k):
        at = self.at
        src = self.ra.at[u, (at.z + k) % at.nz]
        return self.copy(u, 3, src, self.rz.at[u, k - 1], at.zpeer(k))

    def f(self, u):
        ref = self.out.at[u, self.at.p]
        return self.copy(u, 4, ref, ref, self.at.ypeer)

    def f_in(self, u):
        ref = self.out.at[u, 2 * self.at.c + 1 - self.at.y]
        return self.copy(u, 4, ref, ref, self.at.ypeer)

    def g(self, u):
        ref = self.out.at[u, pl.ds(2 * self.at.c, 2)]
        return self.copy(u, 5, ref, ref, self.at.cpeer)

    def g_in(self, u):
        ref = self.out.at[u, pl.ds(2 - 2 * self.at.c, 2)]
        return self.copy(u, 5, ref, ref, self.at.cpeer)

    def either(self, u, what):
        on_x = self.on_x(u)
        pl.when(on_x)(lambda: what(True))
        pl.when(jnp.logical_not(on_x))(lambda: what(False))

    def phase0(self, u):
        self.c(u).start()

    def phase1(self, u):
        at = self.at
        self.c(u).wait_recv()
        add_into(self.rc.at[u % RC], self.grads.at[u % 2, :, :, at.c])
        self.either(u, lambda on_x: self.b(u, on_x).start())

    def phase2(self, u):
        at = self.at
        rc, rb = self.rc.at[u % RC], self.rb.at[u % RB]
        self.b(u, True).wait_recv()

        def add(on_x):
            add_into(rb, rc.at[:, at.x] if on_x else rc.at[:, :, at.y])
            self.a(u, on_x).start()

        self.either(u, add)
        self.b(u, True).wait_send()
        self.c(u).wait_send()

    def phase3(self, u):
        at = self.at
        self.a(u, True).wait_recv()
        turn = jnp.where(self.on_x(u), at.y, at.x)
        add_into(self.ra.at[u], self.rb.at[u % RB, :, turn])
        for k in range(1, at.nz):
            self.z(u, k).start()
        self.a(u, True).wait_send()

    def phase4(self, u):
        at = self.at
        total = self.ra[u, at.z].astype(F32)
        self.copy(u, 3, self.rz.at[u], self.rz.at[u], at.cpeer).wait_recv()
        for k in range(1, at.nz):
            total += self.rz[u, k - 1].astype(F32)
        self.out[u, at.p] = total.astype(BF)
        self.f(u).start()

    def phase5(self, u):
        self.f_in(u).wait_recv()
        self.g(u).start()

    def phase6(self, u):
        self.g_in(u).wait_recv()


PHASES = 7
OFFSETS = (0, 1, 2, 3, 4, 5, 6)


def add_into(dst, src):
    dst[...] = dst[...] + src[...]


class VecSum:
    def __init__(self, shards, reps, gvec, v1, v2, sq, send, recv):
        self.shards, self.reps = shards, reps
        self.r, self.s = lax.axis_index("rep"), lax.axis_index("shard")
        self.row = [{"rep": self.r, "shard": (self.s + k) % shards} for k in range(1, shards)]
        self.col = [{"rep": (self.r + k) % reps, "shard": self.s} for k in range(1, reps)]
        self.gvec, self.v1, self.v2, self.sq = gvec, v1, v2, sq
        self.send, self.recv = send, recv

    @staticmethod
    def sems(shards, reps):
        return 2 * (shards - 1) + reps - 1

    def lanes(self, i):
        return pl.ds(pl.multiple_of(i * 128, 128), 128)

    def copy(self, i, src, dst, peer):
        return remote(src, dst, self.send.at[i], self.recv.at[i], peer)

    def over_shards(self, k):
        src = self.gvec.at[:, self.lanes((self.s + k) % self.shards)]
        return self.copy(k - 1, src, self.v1.at[self.s], self.row[k - 1])

    def over_reps(self, k):
        ref = self.v2.at[self.r]
        return self.copy(self.shards + k - 2, ref, ref, self.col[k - 1])

    def squares(self, k):
        ref = self.sq.at[self.s]
        return self.copy(self.shards + self.reps + k - 3, ref, ref, self.row[k - 1])

    def total(self, ref, count):
        every = ref[0]
        for i in range(1, count):
            every += ref[i]
        return every

    def stage0(self):
        for k in range(1, self.shards):
            self.over_shards(k).start()
        self.v1[self.s] = self.gvec[:, self.lanes(self.s)]

    def stage1(self):
        for k in range(1, self.shards):
            dst = self.v1.at[(self.s + self.shards - k) % self.shards]
            self.copy(k - 1, dst, dst, self.row[k - 1]).wait_recv()
            self.over_shards(k).wait_send()
        self.v2[self.r] = self.total(self.v1, self.shards)
        for k in range(1, self.reps):
            self.over_reps(k).start()

    def stage2(self):
        for k in range(1, self.reps):
            dst = self.v2.at[(self.r + self.reps - k) % self.reps]
            self.copy(self.shards + k - 2, dst, dst, self.col[k - 1]).wait_recv()
            self.over_reps(k).wait_send()
        return self.total(self.v2, self.reps)

    def norm(self, wide, table):
        part = table[:8] * table[:8] + table[8:] * table[8:]
        for i in range(D // 128):
            part += wide[:, i * 128 : i * 128 + 128]
        self.sq[self.s] = part
        for k in range(1, self.shards):
            self.squares(k).start()
        for k in range(1, self.shards):
            i = self.shards + self.reps + k - 3
            dst = self.sq.at[(self.s + self.shards - k) % self.shards]
            self.copy(i, dst, dst, self.row[k - 1]).wait_recv()
            self.squares(k).wait_send()
        return jnp.sqrt(jnp.sum(self.total(self.sq, self.shards), keepdims=True))


def fold_squares(block):
    g = block.astype(F32)
    return jnp.sum((g * g).reshape(-1, 8, D), axis=0)


WIDE = 512


def cols(n, width=WIDE):
    return pl.ds(pl.multiple_of(n * width, width), width)


def tiles(run):
    def one(n, carry):
        run(n)
        return carry

    lax.fori_loop(0, D // WIDE, one, 0)


def back_kernel(
    nz, reps,
    tokens, dy, ht, table, act, full,
    out_hbm, grad_hbm, owned, gtable, norm,
    grad_in, wb, grads, rc, rb, ra, rz, gelu, dact, acc, b1, gb1, gv, wide, v1, v2, sq,
    send, recv, vsend, vrecv, wsem, osem,
):
    at = Place(nz)
    shards = 2 * nz
    fused = reps == 4
    width = FF // shards

    def load(slot, first, second):
        for i, src in enumerate((first, second)):
            pltpu.make_async_copy(src, wb.at[slot, i], wsem.at[slot, i]).start()

    def loaded(slot):
        for i in range(2):
            pltpu.make_async_copy(full.at[0], wb.at[slot, i], wsem.at[slot, i]).wait()

    def load_mlp(j):
        load((j + 2) % 3, full.at[4 + 2 * j], full.at[5 + 2 * j])

    load(0, act.at[0], full.at[0])
    load(2, full.at[4], full.at[5])
    load(1, act.at[1], full.at[1])
    out = wb.at[0, 1]
    out_copy = pltpu.make_async_copy(out, out_hbm, osem.at[0])
    grad_copy = pltpu.make_async_copy(grad_in, grad_hbm, osem.at[1])
    red = Reduce(at, grads, rc, rb, ra, rz, owned, send, recv)
    vecs = VecSum(shards, reps, gv, v1, v2, sq, vsend, vrecv)
    gv[...] = jnp.zeros((VPAD, D), F32)
    wide[...] = jnp.zeros((8, D), F32)
    grad_in[...] = jnp.zeros((LEN, D), F32)
    for j in range(FF // D):
        for s in range(shards):
            f = s * width + j * 128
            b1[j : j + 1, s * 128 : s * 128 + 128] = table[
                6 + f // D : 7 + f // D, f % D : f % D + 128
            ].astype(F32)
    greet(vecs.row + [at.ypeer, at.cpeer, at.diag])

    def write(u, n, value):
        grads[u % 2, :, :, :, :, :, cols(n)] = value.astype(BF).reshape(nz, 2, 2, 2, 32, WIDE)

    def activate(j, half):
        slot = (j + 2) % 3
        parts = [pl.ds(pl.multiple_of(half * 512 + n * 256, 256), 256) for n in range(2)]
        products = []
        for part in parts:
            a = dot(ht[...], wb[slot, 1, :, part], 0, 0)
            products.append((a, dot(dy[...], wb[slot, 0, part, :], 1, 1)))
        for part, (a, dg) in zip(parts, products):
            a = a + b1[pl.ds(j, 1), part]
            square = a * a
            t = jnp.tanh(a * (math.sqrt(2.0 / math.pi) + (math.sqrt(2.0 / math.pi) * 0.044715) * square))
            gate = 0.5 + 0.5 * t
            gelu[j % 2, :, part] = (a * gate).astype(BF)
            slope = gate + a * (1.0 - t * t) * (
                0.5 * math.sqrt(2.0 / math.pi) + (1.5 * 0.044715 * math.sqrt(2.0 / math.pi)) * square
            )
            da = (dg * slope).astype(BF)
            dact[j % 2, :, part] = da
            gb1[pl.ds(j, 1), part] = jnp.sum(da.astype(F32), axis=0, keepdims=True)

    def finish():
        gain = table[0:1].astype(F32)
        shift = table[5:6].astype(F32) + table[10:11].astype(F32)

        def rows_of(i, carry):
            rows = pl.ds(pl.multiple_of(i * 128, 128), 128)
            x = wb[0, 0, rows].astype(F32)
            out[rows] = (x + acc[rows] + shift).astype(BF)
            centered = x - jnp.mean(x, axis=1, keepdims=True)
            rstd = lax.rsqrt(jnp.mean(centered * centered, axis=1, keepdims=True) + 1e-05)
            n = centered * rstd
            dh = grad_in[rows]
            back = dy[rows].astype(F32)
            e = dh * gain
            grad_in[rows] = back + rstd * (
                e
                - jnp.mean(e, axis=1, keepdims=True)
                - n * jnp.mean(e * n, axis=1, keepdims=True)
            )
            gv[0:1] += jnp.sum(dh * n, axis=0, keepdims=True)
            gv[1:2] += jnp.sum(dh, axis=0, keepdims=True)
            gv[5:6] += jnp.sum(back, axis=0, keepdims=True)
            return carry

        lax.fori_loop(0, LEN // 128, rows_of, 0)
        gv[10:11] = gv[5:6]
        for j in range(FF // D):
            for s in range(shards):
                f = s * width + j * 128
                gv[6 + f // D : 7 + f // D, f % D : f % D + 128] = gb1[
                    j : j + 1, s * 128 : s * 128 + 128
                ]

    def tick(t, carry):
        for number in range(1, PHASES):
            u = t - OFFSETS[number]

            def phase(u=u, number=number):
                getattr(red, f"phase{number}")(u)
                if number == PHASES - 1 and fused:
                    wide[...] += fold_squares(owned[u])

            pl.when((u >= 0) & (u < UNITS))(phase)

        dense, qkv = t == 0, (t >= 1) & (t < 4)
        even, odd = t % 2 == 0, t % 2 == 1
        shrink, expand = (t >= 4) & (t < UNITS) & even, (t >= 4) & (t < UNITS) & odd
        again = (t >= 8) & (t < 11)
        slot = t % 2
        j = (t - 4) // 2

        pl.when(t < 4)(lambda: loaded(slot))
        pl.when(t == 1)(lambda: loaded(2))
        pl.when((t == 1) | (t == 2))(lambda: load(1 - slot, act.at[t + 1], full.at[t + 1]))
        pl.when((t == 3) | (t == 4))(lambda: load_mlp(t - 2))
        pl.when(t == 6)(lambda: load_mlp(3))
        pl.when(again)(lambda: load(0, act.at[t - 7], full.at[t - 7]))
        inputs = pltpu.make_async_copy(tokens, wb.at[0, 0], wsem.at[0, 0])
        pl.when(t == 11)(lambda: inputs.start())

        pl.when(dense)(
            lambda: tiles(lambda n: write(t, n, dot(wb[slot, 0], dy[:, cols(n)], 1, 0)))
        )
        pl.when(qkv)(
            lambda: tiles(lambda n: write(t, n, dot(ht[...], wb[slot, 0, cols(n), :], 1, 1)))
        )
        pl.when(shrink)(
            lambda: tiles(lambda n: write(t, n, dot(gelu[j % 2], dy[:, cols(n)], 0, 0)))
        )
        pl.when(expand)(
            lambda: tiles(
                lambda n: write(t, n, dot(ht[...], dact[j % 2, :, cols(n)], 1, 0))
            )
        )
        pl.when(t < UNITS)(lambda: red.phase0(t))

        @pl.when(dense)
        def _():
            def tile(n):
                acc[:, cols(n)] = dot(wb[slot, 0], wb[slot, 1, :, cols(n)], 0, 0)

            tiles(tile)

        ends = (t == UNITS) | (t == UNITS + 1)
        of = jnp.where(ends, t - UNITS + 2, j)

        @pl.when((shrink & (t < 8)) | ends)
        def _():
            def tile(n):
                acc[:, cols(n)] += dot(gelu[of % 2], wb[(of + 2) % 3, 0, :, cols(n)], 1, 0)

            tiles(tile)

        @pl.when((expand & (t < 8)) | ends)
        def _():
            def tile(n):
                grad_in[:, cols(n)] += dot(
                    dact[of % 2], wb[(of + 2) % 3, 1, cols(n), :], 1, 1
                )

            tiles(tile)

        pl.when((t == 3) | (t == 5) | (t == 7))(lambda: loaded((t // 2 + 2) % 3))
        pl.when((t >= 1) & (t < 9))(lambda: activate((t - 1) // 2, 1 - t % 2))

        @pl.when(again)
        def _():
            loaded(0)
            ones = jnp.ones((8, LEN), BF)

            def tile(n):
                grad_in[:, cols(n)] += dot(wb[0, 0], wb[0, 1, cols(n), :], 0, 1)
                gv[pl.ds(t - 6, 1), cols(n)] = dot(ones, wb[0, 0, cols(n), :], 1, 1)[:1]

            tiles(tile)

        @pl.when(t == UNITS + 2)
        def _():
            inputs.wait()
            finish()
            out_copy.start()
            grad_copy.start()

        if fused:
            pl.when(t == UNITS + 3)(vecs.stage0)
            pl.when(t == UNITS + 4)(vecs.stage1)

            @pl.when(t == UNITS + 5)
            def _():
                gtable[...] = vecs.stage2()

        return carry

    lax.fori_loop(0, UNITS + OFFSETS[-1], tick, 0)
    red.finish()
    out_copy.wait()
    grad_copy.wait()
    if fused:
        norm[...] = vecs.norm(wide[...], gtable[...])
    else:
        gtable[...] = gv[...]
        norm[...] = jnp.zeros((1, 1), F32)


def back(tokens, dy, ht, table, act, full, nz, reps):
    shards = 2 * nz
    vcount = VecSum.sems(shards, reps)
    anywhere = pl.BlockSpec(memory_space=pl.ANY)
    inside = pl.BlockSpec(memory_space=pltpu.VMEM)

    def kernel(*refs):
        back_kernel(nz, reps, *refs)

    return pl.pallas_call(
        kernel,
        out_shape=(
            jax.ShapeDtypeStruct((LEN, D), BF),
            jax.ShapeDtypeStruct((LEN, D), F32),
            jax.ShapeDtypeStruct((UNITS, 4, 32, D), BF),
            jax.ShapeDtypeStruct((VPAD, 128 if reps == 4 else D), F32),
            jax.ShapeDtypeStruct((1, 1), F32),
        ),
        in_specs=[anywhere, inside, inside, inside, anywhere, anywhere],
        out_specs=(anywhere, anywhere, inside, inside, inside),
        scratch_shapes=[
            pltpu.VMEM((LEN, D), F32),
            pltpu.VMEM((3, 2, D, D), BF),
            pltpu.VMEM((2, nz, 2, 2, 2, 32, D), BF),
            pltpu.VMEM((RC, nz, 2, 2, 32, D), BF),
            pltpu.VMEM((RB, nz, 2, 32, D), BF),
            pltpu.VMEM((UNITS, nz, 32, D), BF),
            pltpu.VMEM((UNITS, nz - 1, 32, D), BF),
            pltpu.VMEM((2, LEN, D), BF),
            pltpu.VMEM((2, LEN, D), BF),
            pltpu.VMEM((LEN, D), F32),
            pltpu.VMEM((FF // D, D), F32),
            pltpu.VMEM((FF // D, D), F32),
            pltpu.VMEM((VPAD, D), F32),
            pltpu.VMEM((8, D), F32),
            pltpu.VMEM((shards, VPAD, 128), F32),
            pltpu.VMEM((reps, VPAD, 128), F32),
            pltpu.VMEM((shards, 8, 128), F32),
            pltpu.SemaphoreType.DMA((UNITS + 1, Reduce.SEMS)),
            pltpu.SemaphoreType.DMA((UNITS, Reduce.SEMS)),
            pltpu.SemaphoreType.DMA((vcount,)),
            pltpu.SemaphoreType.DMA((vcount,)),
            pltpu.SemaphoreType.DMA((3, 2)),
            pltpu.SemaphoreType.DMA((2,)),
        ],
        compiler_params=pltpu.CompilerParams(
            collective_id=1, has_side_effects=True, vmem_limit_bytes=60 * MIB
        ),
        name="back",
    )(tokens, dy, ht, table, act, full)


def norm_kernel(shards, reps, gvec, own, gtable, norm, v1, v2, sq, send, recv):
    vecs = VecSum(shards, reps, gvec, v1, v2, sq, send, recv)
    greet(vecs.row + vecs.col)
    vecs.stage0()
    wide = lax.fori_loop(
        0, own.shape[0], lambda u, acc: acc + fold_squares(own[u]), jnp.zeros((8, D), F32)
    )
    vecs.stage1()
    gtable[...] = vecs.stage2()
    norm[...] = vecs.norm(wide, gtable[...])


def norm_all(gvec, own, shards, reps):
    count = VecSum.sems(shards, reps)

    def kernel(*refs):
        norm_kernel(shards, reps, *refs)

    inside = pl.BlockSpec(memory_space=pltpu.VMEM)
    return pl.pallas_call(
        kernel,
        out_shape=(
            jax.ShapeDtypeStruct((VPAD, 128), F32),
            jax.ShapeDtypeStruct((1, 1), F32),
        ),
        in_specs=[inside, inside],
        out_specs=(inside, inside),
        scratch_shapes=[
            pltpu.VMEM((shards, VPAD, 128), F32),
            pltpu.VMEM((reps, VPAD, 128), F32),
            pltpu.VMEM((shards, 8, 128), F32),
            pltpu.SemaphoreType.DMA((count,)),
            pltpu.SemaphoreType.DMA((count,)),
        ],
        compiler_params=pltpu.CompilerParams(
            collective_id=2, has_side_effects=True, vmem_limit_bytes=56 * MIB
        ),
        name="norm_all",
    )(gvec, own)


def adamw(master, firsts, seconds, gradient, factor, step_rate, decay_amount):
    clipped = gradient * factor
    momentum = 0.9 * firsts + 0.1 * clipped
    variance = 0.95 * seconds + 0.05 * clipped * clipped
    corrected = momentum / (1.0 - 0.9**STEP)
    spread = variance / (1.0 - 0.95**STEP)
    renewed = master - step_rate * (corrected / (jnp.sqrt(spread) + 1e-08) + decay_amount * master)
    return (momentum, variance, renewed)


def update_kernel(shards, norm, own, own_shrink, gtable, *refs):
    ins, passed, outs, through = refs[:15], refs[15:17], refs[17:32], refs[32:34]
    for src, dst in zip(passed, through):
        dst[...] = src[...]
    factor = jnp.minimum(1.0, clip_limit / (norm[...] + 1e-06))
    width = FF // shards

    def part(number, rows, lanes, gradient):
        trio = ins[3 * number : 3 * number + 3]
        new = adamw(
            *(ref[rows, lanes] for ref in trio), gradient.astype(F32), factor, matrix_rate, decay_rate
        )
        for ref, value in zip(outs[3 * number : 3 * number + 3], new):
            ref[rows, lanes] = value

    every = slice(None)
    for i in range(3):
        part(0, every, slice(i * D, i * D + D), own[1 + i])
    part(1, every, every, own[0])
    for j in range(FF // D):
        for s in range(shards):
            f = s * width + j * 128
            part(2, every, slice(f, f + 128), own[5 + 2 * j, :, s * 128 : s * 128 + 128])
    part(3, every, every, own_shrink[0])

    @pl.when(pl.program_id(0) == 0)
    def _():
        new = adamw(*(ref[...] for ref in ins[12:]), gtable[:VROWS], factor, vector_rate, 0.0)
        for ref, value in zip(outs[12:], new):
            ref[...] = value


def update_all(norm, own, gtable, states, passed, shards):
    steps = 4
    moved = [pl.BlockSpec((LEN // steps, D), lambda i: (i, 0))] * 2
    rows = 128 // steps
    per = steps // 4
    specs = []
    for master in states[:12:3]:
        height, lanes = master.shape
        specs += [pl.BlockSpec((height // steps, lanes), lambda i: (i, 0))] * 3

    specs += [pl.BlockSpec((VROWS, 128), lambda i: (0, 0))] * 3

    def kernel(*refs):
        update_kernel(shards, *refs)

    return pl.pallas_call(
        kernel,
        grid=(steps,),
        out_shape=tuple(jax.ShapeDtypeStruct(a.shape, a.dtype) for a in states + passed),
        in_specs=[
            pl.BlockSpec((1, 1), lambda i: (0, 0)),
            pl.BlockSpec((UNITS, rows, D), lambda i: (0, i, 0)),
            pl.BlockSpec((1, 4 * rows, D), lambda i: (4 + 2 * (i // per), i % per, 0)),
            pl.BlockSpec((VPAD, 128), lambda i: (0, 0)),
        ]
        + specs
        + moved,
        out_specs=tuple(specs + moved),
        compiler_params=pltpu.CompilerParams(vmem_limit_bytes=56 * MIB),
        name="update",
    )(norm, own, own, gtable, *states, *passed)


def body(
    tokens,
    doc_lengths,
    cotangent,
    qkv_weight,
    qkv_firsts,
    qkv_seconds,
    dense_weight,
    dense_firsts,
    dense_seconds,
    expand_weight,
    expand_firsts,
    expand_seconds,
    shrink_weight,
    shrink_firsts,
    shrink_seconds,
    vectors,
    vec_firsts,
    vec_seconds,
    *,
    shards,
    reps,
):
    nz = shards // 2
    vec_own = jnp.pad(vectors.astype(BF).T, ((0, VPAD - VROWS), (0, 0)))
    full, table, ht, act = front(
        doc_lengths, tokens, cotangent, qkv_weight, dense_weight, vec_own, expand_weight, shrink_weight, nz
    )
    output, grad_in, owned, gtable, norm = back(
        tokens, cotangent, ht, table, act, full.reshape(UNITS, D, D), nz, reps
    )
    owned = owned.reshape(UNITS, 128, D)
    if reps != 4:
        quads = [[4 * i + j for i in range(reps // 4)] for j in range(4)]
        owned = lax.psum(owned, "rep", axis_index_groups=quads)
        gtable, norm = norm_all(gtable, owned, shards, reps)
    states = (
        qkv_weight, qkv_firsts, qkv_seconds,
        dense_weight, dense_firsts, dense_seconds,
        expand_weight, expand_firsts, expand_seconds,
        shrink_weight, shrink_firsts, shrink_seconds,
        vectors.T, vec_firsts.T, vec_seconds.T,
    )
    new = tuple(update_all(norm, owned, gtable, states, (output, grad_in), shards))
    return new[15:] + new[:12] + tuple(vec.T for vec in new[12:15]) + (norm.reshape(1),)


def solution(mesh):
    shards, reps = mesh.shape["shard"], mesh.shape["rep"]
    data, state = P(("rep", "shard"), None), P("shard", None)

    def step(*args):
        return body(*args, shards=shards, reps=reps)

    return jax.shard_map(
        step,
        mesh=mesh,
        in_specs=(data, data, data) + (state,) * 15,
        out_specs=(data, data) + (state,) * 15 + (P(),),
        check_vma=False,
    )
```

```python
import math

import jax
import jax.numpy as jnp
from jax import lax
from jax.experimental import pallas as pl
from jax.experimental.pallas import tpu as pltpu
from jax.sharding import PartitionSpec as P

D = 1024
HEADS = 16
HEAD_DIM = 64
ROTARY = 32
FF = 4096
LEN = 1024
STEP = 10
VROWS = 11
VPAD = 16
UNITS = 12
QB = 256

clip_limit = 1.0
matrix_rate = 0.05
vector_rate = 0.8
decay_rate = 0.1

BF = jnp.bfloat16
F32 = jnp.float32
MIB = 1 << 20


def dot(a, b, ca, cb):
    return lax.dot_general(a, b, (((ca,), (cb,)), ((), ())), preferred_element_type=F32)


class Place:
    def __init__(self, nz):
        self.nz = nz
        self.r = lax.axis_index("rep")
        self.s = lax.axis_index("shard")
        self.z, self.x = self.s // 2, self.s % 2
        self.c = self.r % 2
        self.y = (self.r // 2) % 2
        self.p = 2 * self.c + self.y

    def dev(self, r, s):
        return {"rep": r, "shard": s}

    def zpeer(self, k):
        return self.dev(self.r, ((self.z + k) % self.nz) * 2 + self.x)

    @property
    def xpeer(self):
        return self.dev(self.r, self.z * 2 + 1 - self.x)

    @property
    def ypeer(self):
        return self.dev(self.r + 2 - 4 * self.y, self.s)

    @property
    def cpeer(self):
        return self.dev(self.r + 1 - 2 * self.c, self.s)

    @property
    def diag(self):
        return self.dev(self.r + 2 - 4 * self.y + 1 - 2 * self.c, self.s)

    def swap(self, first):
        on_x = self.c == (0 if first else 1)
        return self.dev(
            jnp.where(on_x, self.r, self.r + 2 - 4 * self.y),
            jnp.where(on_x, self.z * 2 + 1 - self.x, self.s),
        )


def greet(peers):
    barrier = pltpu.get_barrier_semaphore()
    for peer in peers:
        pl.semaphore_signal(barrier, inc=1, device_id=peer, device_id_type=pl.DeviceIdType.MESH)
    pl.semaphore_wait(barrier, len(peers))


def remote(src, dst, send, recv, peer):
    return pltpu.make_async_remote_copy(
        src_ref=src,
        dst_ref=dst,
        send_sem=send,
        recv_sem=recv,
        device_id=peer,
        device_id_type=pl.DeviceIdType.MESH,
    )


class Gather:
    STAGES = 5

    def __init__(self, at, own, full, u0, n, lane, width, send, recv, job):
        self.at, self.own, self.full = at, own, full
        self.us, self.lanes = pl.ds(u0, n), pl.ds(lane, width)
        self.send, self.recv, self.job = send, recv, job

    def rows(self, count):
        at = self.at
        return pl.ds(at.c * 64 + at.y * 32, 32) if count == 32 else pl.ds(at.c * 64, 64)

    def part(self, z, x, rows):
        return self.full.at[self.us, z, x, rows, self.lanes]

    def copy(self, i, src, dst, peer):
        return remote(src, dst, self.send.at[self.job, i], self.recv.at[self.job, i], peer)

    def all_of(self, i):
        every = slice(None)
        z, x, count = ((pl.ds(0, self.at.nz - 1), 0, 32), (every, 0, 32), (every, every, 32), (every, every, 64))[i]
        ref = self.part(z, x, pl.ds(0, count))
        return self.copy(i, ref, ref, self.at.cpeer)

    def stage0(self):
        at = self.at
        src = self.own.at[self.us, self.rows(32), self.lanes]
        for k in range(1, at.nz):
            self.copy(0, src, self.part(at.z, at.x, self.rows(32)), at.zpeer(k)).start()

    def stage1(self):
        self.all_of(0).wait_recv()
        ref = self.part(slice(None), self.at.x, self.rows(32))
        self.copy(1, ref, ref, self.at.swap(True)).start()

    def stage2(self):
        at = self.at
        self.all_of(1).wait_recv()
        along_y = self.part(slice(None), slice(None), self.rows(32))
        along_x = self.part(slice(None), at.x, self.rows(64))
        pl.when(at.c == 0)(lambda: self.copy(2, along_y, along_y, at.ypeer).start())
        pl.when(at.c == 1)(lambda: self.copy(2, along_x, along_x, at.xpeer).start())

    def stage3(self):
        self.all_of(2).wait_recv()
        ref = self.part(slice(None), slice(None), self.rows(64))
        self.copy(3, ref, ref, self.at.cpeer).start()

    def stage4(self):
        self.all_of(3).wait_recv()
        for i in range(4):
            self.all_of(i).wait_send()


def rotate_rows(u, cosine, sine):
    top = u[:16] * cosine - u[16:32] * sine
    low = u[16:32] * cosine + u[:16] * sine
    return jnp.concatenate([top, low, u[32:]], axis=0)


def heads_attention(bias, qt, kt, vt, gt, act, dqt, dkt, dvt, pause):
    def scores(head, number):
        q0 = number * QB
        k0 = max(0, number - 2) * QB
        span = q0 + QB - k0
        rows = slice(64 * head, 64 * head + 64)
        q, g = qt[rows, q0 : q0 + QB], gt[rows, q0 : q0 + QB]
        k, v = kt[rows, k0 : k0 + span], vt[rows, k0 : k0 + span]
        return q, g, k, v, dot(k, q, 0, 0) + bias[number, :span], dot(v, g, 0, 0)

    def weigh(head, number, q, g, k, v, s, dp):
        rows = slice(64 * head, 64 * head + 64)
        e = jnp.exp(s - jnp.max(s, axis=0, keepdims=True))
        p = e * (1.0 / jnp.sum(e, axis=0, keepdims=True))
        pb = p.astype(BF)
        o = dot(v, pb, 1, 0)
        inner = jnp.sum(o * g.astype(F32), axis=0, keepdims=True)
        ds = (p * (dp - inner)).astype(BF)
        act[0, rows, number * QB : number * QB + QB] = o.astype(BF)
        return q, g, k, pb, ds

    def spread(head, number, q, g, k, pb, ds):
        q0 = number * QB
        k0 = max(0, number - 2) * QB
        old = q0 - k0
        rows = slice(64 * head, 64 * head + 64)
        dqt[rows, q0 : q0 + QB] = dot(k, ds, 1, 0)
        dk = dot(q, ds, 1, 1)
        dv = dot(g, pb, 1, 1)
        if old:
            dkt[rows, k0:q0] += dk[:, :old]
            dvt[rows, k0:q0] += dv[:, :old]
        dkt[rows, q0 : q0 + QB] = dk[:, old:]
        dvt[rows, q0 : q0 + QB] = dv[:, old:]

    order = [(head, number) for number in range(LEN // QB) for head in range(4)]
    ready, waiting = scores(*order[0]), None
    for i, (head, number) in enumerate(order):
        following = scores(*order[i + 1]) if i + 1 < len(order) else None
        weighed = weigh(head, number, *ready)
        if waiting is not None:
            spread(*waiting)
        waiting, ready = (head, number, *weighed), following
        if i % 4 == 3:
            pause(i // 4)
    spread(*waiting)


JOBS = UNITS + 1
READY = 6
LAGS = (0, 1, 2, 4, 5)


def run_stage(gather, stage):
    getattr(gather, f"stage{stage}")()


def front_kernel(
    nz,
    lengths, tokens_hbm, dy_hbm, wqkv, wd, vec, wexpand, wshrink,
    full, table, ht_hbm, act_hbm,
    tokens, dy, ht, act, own, expand_f, shrink_f, wd_v, wq_v, bias, cosine, sine, qt, kt, vt, gt, dqf, dkf, dvf,
    send, recv, vsend, vrecv, lsem,
):
    at = Place(nz)
    shards = 2 * nz
    others = [at.dev(at.r, (at.s + k) % shards) for k in range(1, shards)]
    load_expand = pltpu.make_async_copy(wexpand, expand_f, lsem.at[0])
    load_shrink = pltpu.make_async_copy(wshrink, shrink_f, lsem.at[1])
    load_tokens = pltpu.make_async_copy(tokens_hbm, tokens, lsem.at[7])
    load_dy = pltpu.make_async_copy(dy_hbm, dy, lsem.at[8])
    store_ht = pltpu.make_async_copy(ht, ht_hbm, lsem.at[9])
    for load in (load_tokens, load_dy, load_expand, load_shrink):
        load.start()
    own[0] = wd[...].astype(BF)
    for i in range(3):
        own[1 + i] = wqkv[:, i * D : i * D + D].astype(BF)
    greet(others + [at.ypeer, at.cpeer])

    def lanes(i):
        return pl.ds(pl.multiple_of(i * 128, 128), 128)

    vcopies = [
        remote(vec, table.at[:, lanes(at.s)], vsend.at[k], vrecv.at[k], peer)
        for k, peer in enumerate(others)
    ]
    for copy in vcopies:
        copy.start()
    table[:, lanes(at.s)] = vec[...]
    mine = pl.ds(at.p * 32, 32)
    local_a = pltpu.make_async_copy(
        own.at[0:4, mine], full.at[0:4, at.z, at.x, mine], lsem.at[2]
    )
    local_a.start()
    local_f = pltpu.make_async_copy(
        own.at[4:UNITS, mine], full.at[4:UNITS, at.z, at.x, mine], lsem.at[3]
    )

    def cast_rest():
        load_expand.wait()
        load_shrink.wait()
        width = FF // shards
        for j in range(FF // D):
            own[4 + 2 * j] = shrink_f[j * 128 : j * 128 + 128].astype(BF)
            for b in range(shards):
                own[5 + 2 * j, :, b * 128 : b * 128 + 128] = expand_f[
                    :, b * width + j * 128 : b * width + j * 128 + 128
                ].astype(BF)
        local_f.start()

    def tables():
        place = lax.broadcasted_iota(jnp.int32, (1, LEN), 1)
        start = jnp.zeros((1, LEN), jnp.int32)
        end = 0
        for d in range(lengths.shape[1]):
            end = end + lengths[0, d]
            start = start + jnp.where(place >= end, lengths[0, d], 0)
        m = lax.broadcasted_iota(jnp.int32, (ROTARY // 2, LEN), 0).astype(F32)
        frequency = jnp.exp(m * (-2.0 * math.log(10000.0) / ROTARY))
        angle = (place - start).astype(F32) * frequency
        cosine[...] = jnp.cos(angle)
        sine[...] = jnp.sin(angle)
        for number in range(LEN // QB):
            q0 = number * QB
            k0 = max(0, number - 2) * QB
            span = q0 + QB - k0
            j = k0 + lax.broadcasted_iota(jnp.int32, (span, QB), 0)
            i = q0 + lax.broadcasted_iota(jnp.int32, (span, QB), 1)
            allowed = (j >= start[:, q0 : q0 + QB]) & (j <= i)
            bias[number, :span] = jnp.where(allowed, 0.0, -1e30)

    def wait_vec():
        for k, copy in enumerate(vcopies):
            came = (at.s + shards - (k + 1)) % shards
            remote(vec, table.at[:, lanes(came)], vsend.at[k], vrecv.at[k], others[k]).wait_recv()
            copy.wait_send()

    def norm_rows(i):
        rows = pl.ds(pl.multiple_of(i * 256, 256), 256)
        x = tokens[rows].astype(F32)
        centered = x - jnp.mean(x, axis=1, keepdims=True)
        scaled = centered * lax.rsqrt(jnp.mean(centered * centered, axis=1, keepdims=True) + 1e-05)
        h = scaled * table[0:1].astype(F32) + table[1:2].astype(F32)
        ht[:, rows] = h.astype(BF).T

    def part(job, stage):
        args = (send, recv, job)
        if isinstance(job, int):
            if job == 1:
                gather = Gather(at, own, full, 0, 1, 0, D, *args)
            elif job < 5:
                gather = Gather(at, own, full, 1, 3, 256 * max(0, job - 1), 256, *args)
            else:
                gather = Gather(at, own, full, job - 1, 1, 0, D, *args)
            run_stage(gather, stage)
            return
        lane = pl.multiple_of((job - 1) * 256, 256)
        pl.when((job >= 2) & (job < 5))(
            lambda: run_stage(Gather(at, own, full, 1, 3, lane, 256, *args), stage)
        )
        pl.when((job >= 5) & (job < JOBS))(
            lambda: run_stage(Gather(at, own, full, job - 1, 1, 0, D, *args), stage)
        )

    def load_quad(quad):
        lane = quad * 256 if isinstance(quad, int) else pl.multiple_of(quad * 256, 256)
        src = full.at[pl.ds(1, 3), :, :, :, pl.ds(lane, 256)]
        return pltpu.make_async_copy(src, wq_v.at[quad % 2], lsem.at[4 + quad % 2])

    load_dense = pltpu.make_async_copy(full.at[0], wd_v, lsem.at[6])
    side = {
        0: (tables,),
        1: (wait_vec, load_tokens.wait, lambda: norm_rows(0)),
        2: (lambda: norm_rows(1), lambda: norm_rows(2)),
        3: (lambda: norm_rows(3), store_ht.start),
        4: (cast_rest,),
    }
    for step in range(READY):
        for stage in range(Gather.STAGES):
            if 0 <= step - stage < 2:
                if step == 1 and stage == 1:
                    local_a.wait()
                part(step - stage, stage)
            if step - LAGS[stage] >= 2:
                part(step - LAGS[stage], stage)
        for what in side.get(step, ()):
            what()
        if step == 4:
            load_quad(0).start()
    load_dense.start()
    local_f.wait()

    def prepare(quad):
        cols = pl.ds(pl.multiple_of(quad * 256, 256), 256)
        load_quad(quad).wait()
        pl.when(quad == 0)(load_dense.wait)
        pl.when(quad == 0)(load_dy.wait)
        for part, dst in enumerate((qt, kt, vt)):
            w = wq_v[quad % 2, part].reshape(D, 256)
            u = dot(w, ht[...], 0, 0)
            ones = jnp.ones((1, 128), BF)
            b = dot(table[2 + part : 3 + part, cols], ones, 0, 0)[:, :1]
            u = u + b
            if part == 2:
                dst[...] = u.astype(BF)
                continue
            for head in range(4):
                turned = rotate_rows(u[head * 64 : head * 64 + 64], cosine[...], sine[...])
                if part == 0:
                    turned = turned * (1.0 / math.sqrt(HEAD_DIM))
                dst[head * 64 : head * 64 + 64] = turned.astype(BF)
        for half in range(2):
            w = wd_v[quad, half]
            gt[half * 128 : half * 128 + 128] = dot(w, dy[...], 1, 1).astype(BF)

    def store_act(quad):
        rows = pl.ds(pl.multiple_of(quad * 256, 256), 256)
        return pltpu.make_async_copy(act.at[quad % 2], act_hbm.at[:, rows], lsem.at[10 + quad % 2])

    def one_quad(quad, carry):
        prepare(quad)
        pl.when(quad >= 2)(lambda: store_act(quad - 2).wait())
        here = act.at[quad % 2]

        def pause(number):
            i, left = quad * 4 + number, JOBS + LAGS[-1] - READY
            before, after = ((n * left + HEADS - 1) // HEADS for n in (i, i + 1))

            @pl.when(after > before)
            def _():
                for stage, lag in enumerate(LAGS):
                    part(READY + before - lag, stage)

            if number == 2:
                pl.when(quad < 3)(lambda: load_quad(quad + 1).start())

        heads_attention(bias, qt, kt, vt, gt, here, dqf, dkf, dvf, pause)
        for head in range(4):
            rows = slice(64 * head, 64 * head + 64)
            back = rotate_rows(dqf[rows], cosine[...], -sine[...]) * (1.0 / math.sqrt(HEAD_DIM))
            here[1, rows] = back.astype(BF)
            here[2, rows] = rotate_rows(dkf[rows], cosine[...], -sine[...]).astype(BF)
            here[3, rows] = dvf[rows].astype(BF)
        store_act(quad).start()
        return carry

    lax.fori_loop(0, 4, one_quad, 0)
    for quad in (2, 3):
        store_act(quad).wait()
    store_ht.wait()


def front(lengths, tokens, dy, wqkv, wd, vec, wexpand, wshrink, nz):
    shards = 2 * nz
    anywhere = pl.BlockSpec(memory_space=pl.ANY)
    inside = pl.BlockSpec(memory_space=pltpu.VMEM)

    def kernel(*refs):
        front_kernel(nz, *refs)

    return pl.pallas_call(
        kernel,
        out_shape=(
            jax.ShapeDtypeStruct((UNITS, nz, 2, 128, D), BF),
            jax.ShapeDtypeStruct((VPAD, D), BF),
            jax.ShapeDtypeStruct((D, LEN), BF),
            jax.ShapeDtypeStruct((4, D, LEN), BF),
        ),
        in_specs=[
            pl.BlockSpec(memory_space=pltpu.SMEM),
            anywhere,
            anywhere,
            inside,
            inside,
            inside,
            anywhere,
            anywhere,
        ],
        out_specs=(anywhere, inside, anywhere, anywhere),
        scratch_shapes=[
            pltpu.VMEM((LEN, D), BF),
            pltpu.VMEM((LEN, D), BF),
            pltpu.VMEM((D, LEN), BF),
            pltpu.VMEM((2, 4, 256, LEN), BF),
            pltpu.VMEM((UNITS, 128, D), BF),
            pltpu.VMEM(wexpand.shape, F32),
            pltpu.VMEM(wshrink.shape, F32),
            pltpu.VMEM((nz, 2, 128, D), BF),
            pltpu.VMEM((2, 3, nz, 2, 128, 256), BF),
            pltpu.VMEM((LEN // QB, 3 * QB, QB), F32),
            pltpu.VMEM((ROTARY // 2, LEN), F32),
            pltpu.VMEM((ROTARY // 2, LEN), F32),
            pltpu.VMEM((256, LEN), BF),
            pltpu.VMEM((256, LEN), BF),
            pltpu.VMEM((256, LEN), BF),
            pltpu.VMEM((256, LEN), BF),
            pltpu.VMEM((256, LEN), F32),
            pltpu.VMEM((256, LEN), F32),
            pltpu.VMEM((256, LEN), F32),
            pltpu.SemaphoreType.DMA((JOBS, 4)),
            pltpu.SemaphoreType.DMA((JOBS, 4)),
            pltpu.SemaphoreType.DMA((shards - 1,)),
            pltpu.SemaphoreType.DMA((shards - 1,)),
            pltpu.SemaphoreType.DMA((12,)),
        ],
        compiler_params=pltpu.CompilerParams(
            collective_id=0, has_side_effects=True, vmem_limit_bytes=58 * MIB
        ),
        name="front",
    )(lengths, tokens, dy, wqkv, wd, vec, wexpand, wshrink)


RC, RB = 3, 6


class Reduce:
    def __init__(self, at, grads, rc, rb, ra, rz, out, send, recv):
        self.at = at
        self.grads, self.rc, self.rb, self.ra, self.rz, self.out = grads, rc, rb, ra, rz, out
        self.send, self.recv = send, recv

    SEMS = 6

    def copy(self, u, i, src, dst, peer):
        send = self.send.at[u, i] if i < 3 else self.send.at[UNITS, i]
        return remote(src, dst, send, self.recv.at[u, i], peer)

    def finish(self):
        pieces = self.out.at[:, pl.ds(0, 1)], self.out.at[:, pl.ds(0, 2)]
        for i, ref in enumerate((self.rz,) + pieces):
            remote(ref, ref, self.send.at[UNITS, 3 + i], self.recv.at[0, 3 + i], self.at.cpeer).wait_send()

    def c(self, u):
        at = self.at
        return self.copy(u, 0, self.grads.at[u % 2, :, :, 1 - at.c], self.rc.at[u % RC], at.cpeer)

    def on_x(self, u):
        return (self.at.c == 1) | (u % 4 == 3)

    def b(self, u, on_x):
        at = self.at
        rc = self.rc.at[u % RC]
        src = rc.at[:, 1 - at.x] if on_x else rc.at[:, :, 1 - at.y]
        return self.copy(u, 1, src, self.rb.at[u % RB], at.xpeer if on_x else at.ypeer)

    def a(self, u, on_x):
        at = self.at
        src = self.rb.at[u % RB, :, 1 - (at.y if on_x else at.x)]
        return self.copy(u, 2, src, self.ra.at[u], at.ypeer if on_x else at.xpeer)

    def z(self, u, k):
        at = self.at
        src = self.ra.at[u, (at.z + k) % at.nz]
        return self.copy(u, 3, src, self.rz.at[u, k - 1], at.zpeer(k))

    def f(self, u):
        ref = self.out.at[u, self.at.p]
        return self.copy(u, 4, ref, ref, self.at.ypeer)

    def f_in(self, u):
        ref = self.out.at[u, 2 * self.at.c + 1 - self.at.y]
        return self.copy(u, 4, ref, ref, self.at.ypeer)

    def g(self, u):
        ref = self.out.at[u, pl.ds(2 * self.at.c, 2)]
        return self.copy(u, 5, ref, ref, self.at.cpeer)

    def g_in(self, u):
        ref = self.out.at[u, pl.ds(2 - 2 * self.at.c, 2)]
        return self.copy(u, 5, ref, ref, self.at.cpeer)

    def either(self, u, what):
        on_x = self.on_x(u)
        pl.when(on_x)(lambda: what(True))
        pl.when(jnp.logical_not(on_x))(lambda: what(False))

    def phase0(self, u):
        self.c(u).start()

    def phase1(self, u):
        at = self.at
        self.c(u).wait_recv()
        add_into(self.rc.at[u % RC], self.grads.at[u % 2, :, :, at.c])
        self.either(u, lambda on_x: self.b(u, on_x).start())

    def phase2(self, u):
        at = self.at
        rc, rb = self.rc.at[u % RC], self.rb.at[u % RB]
        self.b(u, True).wait_recv()

        def add(on_x):
            add_into(rb, rc.at[:, at.x] if on_x else rc.at[:, :, at.y])
            self.a(u, on_x).start()

        self.either(u, add)
        self.b(u, True).wait_send()
        self.c(u).wait_send()

    def phase3(self, u):
        at = self.at
        self.a(u, True).wait_recv()
        turn = jnp.where(self.on_x(u), at.y, at.x)
        add_into(self.ra.at[u], self.rb.at[u % RB, :, turn])
        for k in range(1, at.nz):
            self.z(u, k).start()
        self.a(u, True).wait_send()

    def phase4(self, u):
        at = self.at
        total = self.ra[u, at.z].astype(F32)
        self.copy(u, 3, self.rz.at[u], self.rz.at[u], at.cpeer).wait_recv()
        for k in range(1, at.nz):
            total += self.rz[u, k - 1].astype(F32)
        self.out[u, at.p] = total.astype(BF)
        self.f(u).start()

    def phase5(self, u):
        self.f_in(u).wait_recv()
        self.g(u).start()

    def phase6(self, u):
        self.g_in(u).wait_recv()


PHASES = 7
OFFSETS = (0, 1, 2, 3, 4, 5, 6)


def add_into(dst, src):
    dst[...] = dst[...] + src[...]


class VecSum:
    def __init__(self, shards, reps, gvec, v1, v2, sq, send, recv):
        self.shards, self.reps = shards, reps
        self.r, self.s = lax.axis_index("rep"), lax.axis_index("shard")
        self.row = [{"rep": self.r, "shard": (self.s + k) % shards} for k in range(1, shards)]
        self.col = [{"rep": (self.r + k) % reps, "shard": self.s} for k in range(1, reps)]
        self.gvec, self.v1, self.v2, self.sq = gvec, v1, v2, sq
        self.send, self.recv = send, recv

    @staticmethod
    def sems(shards, reps):
        return 2 * (shards - 1) + reps - 1

    def lanes(self, i):
        return pl.ds(pl.multiple_of(i * 128, 128), 128)

    def copy(self, i, src, dst, peer):
        return remote(src, dst, self.send.at[i], self.recv.at[i], peer)

    def over_shards(self, k):
        src = self.gvec.at[:, self.lanes((self.s + k) % self.shards)]
        return self.copy(k - 1, src, self.v1.at[self.s], self.row[k - 1])

    def over_reps(self, k):
        ref = self.v2.at[self.r]
        return self.copy(self.shards + k - 2, ref, ref, self.col[k - 1])

    def squares(self, k):
        ref = self.sq.at[self.s]
        return self.copy(self.shards + self.reps + k - 3, ref, ref, self.row[k - 1])

    def total(self, ref, count):
        every = ref[0]
        for i in range(1, count):
            every += ref[i]
        return every

    def stage0(self):
        for k in range(1, self.shards):
            self.over_shards(k).start()
        self.v1[self.s] = self.gvec[:, self.lanes(self.s)]

    def stage1(self):
        for k in range(1, self.shards):
            dst = self.v1.at[(self.s + self.shards - k) % self.shards]
            self.copy(k - 1, dst, dst, self.row[k - 1]).wait_recv()
            self.over_shards(k).wait_send()
        self.v2[self.r] = self.total(self.v1, self.shards)
        for k in range(1, self.reps):
            self.over_reps(k).start()

    def stage2(self):
        for k in range(1, self.reps):
            dst = self.v2.at[(self.r + self.reps - k) % self.reps]
            self.copy(self.shards + k - 2, dst, dst, self.col[k - 1]).wait_recv()
            self.over_reps(k).wait_send()
        return self.total(self.v2, self.reps)

    def norm(self, wide, table):
        part = table[:8] * table[:8] + table[8:] * table[8:]
        for i in range(D // 128):
            part += wide[:, i * 128 : i * 128 + 128]
        self.sq[self.s] = part
        for k in range(1, self.shards):
            self.squares(k).start()
        for k in range(1, self.shards):
            i = self.shards + self.reps + k - 3
            dst = self.sq.at[(self.s + self.shards - k) % self.shards]
            self.copy(i, dst, dst, self.row[k - 1]).wait_recv()
            self.squares(k).wait_send()
        return jnp.sqrt(jnp.sum(self.total(self.sq, self.shards), keepdims=True))


def fold_squares(block):
    g = block.astype(F32)
    return jnp.sum((g * g).reshape(-1, 8, D), axis=0)


WIDE = 512


def cols(n, width=WIDE):
    return pl.ds(pl.multiple_of(n * width, width), width)


def tiles(run):
    def one(n, carry):
        run(n)
        return carry

    lax.fori_loop(0, D // WIDE, one, 0)


def back_kernel(
    nz, reps,
    tokens, dy_hbm, ht_hbm, table, act, full,
    out_hbm, grad_hbm, owned, gtable, norm,
    dy, ht, grad_in, wb, grads, rc, rb, ra, rz, gelu, dact, acc, b1, gb1, gv, wide, v1, v2, sq,
    send, recv, vsend, vrecv, wsem, osem,
):
    at = Place(nz)
    shards = 2 * nz
    fused = reps == 4
    width = FF // shards

    def load(slot, first, second):
        for i, src in enumerate((first, second)):
            pltpu.make_async_copy(src, wb.at[slot, i], wsem.at[slot, i]).start()

    def loaded(slot):
        for i in range(2):
            pltpu.make_async_copy(full.at[0], wb.at[slot, i], wsem.at[slot, i]).wait()

    def load_mlp(j):
        load((j + 2) % 3, full.at[4 + 2 * j], full.at[5 + 2 * j])

    load_dy = pltpu.make_async_copy(dy_hbm, dy, osem.at[2])
    load_ht = pltpu.make_async_copy(ht_hbm, ht, osem.at[3])
    load_dy.start()
    load(0, act.at[0], full.at[0])
    load_ht.start()
    load(2, full.at[4], full.at[5])
    load(1, act.at[1], full.at[1])
    out = wb.at[0, 1]
    out_copy = pltpu.make_async_copy(out, out_hbm, osem.at[0])
    grad_copy = pltpu.make_async_copy(grad_in, grad_hbm, osem.at[1])
    red = Reduce(at, grads, rc, rb, ra, rz, owned, send, recv)
    vecs = VecSum(shards, reps, gv, v1, v2, sq, vsend, vrecv)
    gv[...] = jnp.zeros((VPAD, D), F32)
    wide[...] = jnp.zeros((8, D), F32)
    grad_in[...] = jnp.zeros((LEN, D), F32)
    for j in range(FF // D):
        for s in range(shards):
            f = s * width + j * 128
            b1[j : j + 1, s * 128 : s * 128 + 128] = table[
                6 + f // D : 7 + f // D, f % D : f % D + 128
            ].astype(F32)
    greet(vecs.row + [at.ypeer, at.cpeer, at.diag])

    def write(u, n, value):
        grads[u % 2, :, :, :, :, :, cols(n)] = value.astype(BF).reshape(nz, 2, 2, 2, 32, WIDE)

    def activate(j, half):
        slot = (j + 2) % 3
        parts = [pl.ds(pl.multiple_of(half * 512 + n * 256, 256), 256) for n in range(2)]
        products = []
        for part in parts:
            a = dot(ht[...], wb[slot, 1, :, part], 0, 0)
            products.append((a, dot(dy[...], wb[slot, 0, part, :], 1, 1)))
        for part, (a, dg) in zip(parts, products):
            a = a + b1[pl.ds(j, 1), part]
            square = a * a
            t = jnp.tanh(a * (math.sqrt(2.0 / math.pi) + (math.sqrt(2.0 / math.pi) * 0.044715) * square))
            gate = 0.5 + 0.5 * t
            gelu[j % 2, :, part] = (a * gate).astype(BF)
            slope = gate + a * (1.0 - t * t) * (
                0.5 * math.sqrt(2.0 / math.pi) + (1.5 * 0.044715 * math.sqrt(2.0 / math.pi)) * square
            )
            da = (dg * slope).astype(BF)
            dact[j % 2, :, part] = da
            gb1[pl.ds(j, 1), part] = jnp.sum(da.astype(F32), axis=0, keepdims=True)

    def finish():
        gain = table[0:1].astype(F32)
        shift = table[5:6].astype(F32) + table[10:11].astype(F32)

        def rows_of(i, carry):
            rows = pl.ds(pl.multiple_of(i * 128, 128), 128)
            x = wb[0, 0, rows].astype(F32)
            out[rows] = (x + acc[rows] + shift).astype(BF)
            centered = x - jnp.mean(x, axis=1, keepdims=True)
            rstd = lax.rsqrt(jnp.mean(centered * centered, axis=1, keepdims=True) + 1e-05)
            n = centered * rstd
            dh = grad_in[rows]
            back = dy[rows].astype(F32)
            e = dh * gain
            grad_in[rows] = back + rstd * (
                e
                - jnp.mean(e, axis=1, keepdims=True)
                - n * jnp.mean(e * n, axis=1, keepdims=True)
            )
            gv[0:1] += jnp.sum(dh * n, axis=0, keepdims=True)
            gv[1:2] += jnp.sum(dh, axis=0, keepdims=True)
            gv[5:6] += jnp.sum(back, axis=0, keepdims=True)
            return carry

        lax.fori_loop(0, LEN // 128, rows_of, 0)
        gv[10:11] = gv[5:6]
        for j in range(FF // D):
            for s in range(shards):
                f = s * width + j * 128
                gv[6 + f // D : 7 + f // D, f % D : f % D + 128] = gb1[
                    j : j + 1, s * 128 : s * 128 + 128
                ]

    def tick(t, carry):
        for number in range(1, PHASES):
            u = t - OFFSETS[number]

            def phase(u=u, number=number):
                getattr(red, f"phase{number}")(u)
                if number == PHASES - 1 and fused:
                    wide[...] += fold_squares(owned[u])

            pl.when((u >= 0) & (u < UNITS))(phase)

        dense, qkv = t == 0, (t >= 1) & (t < 4)
        even, odd = t % 2 == 0, t % 2 == 1
        shrink, expand = (t >= 4) & (t < UNITS) & even, (t >= 4) & (t < UNITS) & odd
        again = (t >= 9) & (t < 12)
        slot = t % 2
        j = (t - 4) // 2

        pl.when(t < 4)(lambda: loaded(slot))
        pl.when(t == 0)(load_dy.wait)
        pl.when(t == 1)(load_ht.wait)
        pl.when(t == 1)(lambda: loaded(2))
        pl.when((t == 1) | (t == 2))(lambda: load(1 - slot, act.at[t + 1], full.at[t + 1]))
        pl.when((t == 3) | (t == 4))(lambda: load_mlp(t - 2))
        pl.when(t == 6)(lambda: load_mlp(3))
        pl.when(again)(lambda: load(0, act.at[t - 8], full.at[t - 8]))
        inputs = pltpu.make_async_copy(tokens, wb.at[0, 0], wsem.at[0, 0])
        pl.when(t == 12)(lambda: inputs.start())

        pl.when(dense)(
            lambda: tiles(lambda n: write(t, n, dot(wb[slot, 0], dy[:, cols(n)], 1, 0)))
        )
        pl.when(qkv)(
            lambda: tiles(lambda n: write(t, n, dot(ht[...], wb[slot, 0, cols(n), :], 1, 1)))
        )
        pl.when(shrink)(
            lambda: tiles(lambda n: write(t, n, dot(gelu[j % 2], dy[:, cols(n)], 0, 0)))
        )
        pl.when(expand)(
            lambda: tiles(
                lambda n: write(t, n, dot(ht[...], dact[j % 2, :, cols(n)], 1, 0))
            )
        )
        pl.when(t < UNITS)(lambda: red.phase0(t))

        @pl.when(dense)
        def _():
            def tile(n):
                acc[:, cols(n)] = dot(wb[slot, 0], wb[slot, 1, :, cols(n)], 0, 0)

            tiles(tile)

        ends = (t == UNITS) | (t == UNITS + 1)
        of = jnp.where(ends, t - UNITS + 2, j)

        @pl.when((shrink & (t < 8)) | ends)
        def _():
            def tile(n):
                acc[:, cols(n)] += dot(gelu[of % 2], wb[(of + 2) % 3, 0, :, cols(n)], 1, 0)

            tiles(tile)

        @pl.when((expand & (t < 8)) | ends)
        def _():
            def tile(n):
                grad_in[:, cols(n)] += dot(
                    dact[of % 2], wb[(of + 2) % 3, 1, cols(n), :], 1, 1
                )

            tiles(tile)

        pl.when((t == 3) | (t == 5) | (t == 7))(lambda: loaded((t // 2 + 2) % 3))
        pl.when((t >= 1) & (t < 9))(lambda: activate((t - 1) // 2, 1 - t % 2))

        @pl.when(again)
        def _():
            loaded(0)
            ones = jnp.ones((8, LEN), BF)

            def tile(n):
                grad_in[:, cols(n)] += dot(wb[0, 0], wb[0, 1, cols(n), :], 0, 1)
                gv[pl.ds(t - 7, 1), cols(n)] = dot(ones, wb[0, 0, cols(n), :], 1, 1)[:1]

            tiles(tile)

        @pl.when(t == UNITS + 2)
        def _():
            inputs.wait()
            finish()
            out_copy.start()
            grad_copy.start()

        if fused:
            pl.when(t == UNITS + 3)(vecs.stage0)
            pl.when(t == UNITS + 4)(vecs.stage1)

            @pl.when(t == UNITS + 5)
            def _():
                gtable[...] = vecs.stage2()

        return carry

    lax.fori_loop(0, UNITS + OFFSETS[-1], tick, 0)
    red.finish()
    out_copy.wait()
    grad_copy.wait()
    if fused:
        norm[...] = vecs.norm(wide[...], gtable[...])
    else:
        gtable[...] = gv[...]
        norm[...] = jnp.zeros((1, 1), F32)


def back(tokens, dy, ht, table, act, full, nz, reps):
    shards = 2 * nz
    vcount = VecSum.sems(shards, reps)
    anywhere = pl.BlockSpec(memory_space=pl.ANY)
    inside = pl.BlockSpec(memory_space=pltpu.VMEM)

    def kernel(*refs):
        back_kernel(nz, reps, *refs)

    return pl.pallas_call(
        kernel,
        out_shape=(
            jax.ShapeDtypeStruct((LEN, D), BF),
            jax.ShapeDtypeStruct((LEN, D), F32),
            jax.ShapeDtypeStruct((UNITS, 4, 32, D), BF),
            jax.ShapeDtypeStruct((VPAD, 128 if reps == 4 else D), F32),
            jax.ShapeDtypeStruct((1, 1), F32),
        ),
        in_specs=[anywhere, anywhere, anywhere, inside, anywhere, anywhere],
        out_specs=(anywhere, anywhere, inside, inside, inside),
        scratch_shapes=[
            pltpu.VMEM((LEN, D), BF),
            pltpu.VMEM((D, LEN), BF),
            pltpu.VMEM((LEN, D), F32),
            pltpu.VMEM((3, 2, D, D), BF),
            pltpu.VMEM((2, nz, 2, 2, 2, 32, D), BF),
            pltpu.VMEM((RC, nz, 2, 2, 32, D), BF),
            pltpu.VMEM((RB, nz, 2, 32, D), BF),
            pltpu.VMEM((UNITS, nz, 32, D), BF),
            pltpu.VMEM((UNITS, nz - 1, 32, D), BF),
            pltpu.VMEM((2, LEN, D), BF),
            pltpu.VMEM((2, LEN, D), BF),
            pltpu.VMEM((LEN, D), F32),
            pltpu.VMEM((FF // D, D), F32),
            pltpu.VMEM((FF // D, D), F32),
            pltpu.VMEM((VPAD, D), F32),
            pltpu.VMEM((8, D), F32),
            pltpu.VMEM((shards, VPAD, 128), F32),
            pltpu.VMEM((reps, VPAD, 128), F32),
            pltpu.VMEM((shards, 8, 128), F32),
            pltpu.SemaphoreType.DMA((UNITS + 1, Reduce.SEMS)),
            pltpu.SemaphoreType.DMA((UNITS, Reduce.SEMS)),
            pltpu.SemaphoreType.DMA((vcount,)),
            pltpu.SemaphoreType.DMA((vcount,)),
            pltpu.SemaphoreType.DMA((3, 2)),
            pltpu.SemaphoreType.DMA((4,)),
        ],
        compiler_params=pltpu.CompilerParams(
            collective_id=1, has_side_effects=True, vmem_limit_bytes=60 * MIB
        ),
        name="back",
    )(tokens, dy, ht, table, act, full)


def norm_kernel(shards, reps, gvec, own, gtable, norm, v1, v2, sq, send, recv):
    vecs = VecSum(shards, reps, gvec, v1, v2, sq, send, recv)
    greet(vecs.row + vecs.col)
    vecs.stage0()
    wide = lax.fori_loop(
        0, own.shape[0], lambda u, acc: acc + fold_squares(own[u]), jnp.zeros((8, D), F32)
    )
    vecs.stage1()
    gtable[...] = vecs.stage2()
    norm[...] = vecs.norm(wide, gtable[...])


def norm_all(gvec, own, shards, reps):
    count = VecSum.sems(shards, reps)

    def kernel(*refs):
        norm_kernel(shards, reps, *refs)

    inside = pl.BlockSpec(memory_space=pltpu.VMEM)
    return pl.pallas_call(
        kernel,
        out_shape=(
            jax.ShapeDtypeStruct((VPAD, 128), F32),
            jax.ShapeDtypeStruct((1, 1), F32),
        ),
        in_specs=[inside, inside],
        out_specs=(inside, inside),
        scratch_shapes=[
            pltpu.VMEM((shards, VPAD, 128), F32),
            pltpu.VMEM((reps, VPAD, 128), F32),
            pltpu.VMEM((shards, 8, 128), F32),
            pltpu.SemaphoreType.DMA((count,)),
            pltpu.SemaphoreType.DMA((count,)),
        ],
        compiler_params=pltpu.CompilerParams(
            collective_id=2, has_side_effects=True, vmem_limit_bytes=56 * MIB
        ),
        name="norm_all",
    )(gvec, own)


def adamw(master, firsts, seconds, gradient, factor, step_rate, decay_amount):
    clipped = gradient * factor
    momentum = 0.9 * firsts + 0.1 * clipped
    variance = 0.95 * seconds + 0.05 * clipped * clipped
    corrected = momentum / (1.0 - 0.9**STEP)
    spread = variance / (1.0 - 0.95**STEP)
    renewed = master - step_rate * (corrected / (jnp.sqrt(spread) + 1e-08) + decay_amount * master)
    return (momentum, variance, renewed)


def update_kernel(shards, norm, own, gtable, *refs):
    ins, outs, bufs, sin, sout = refs[:17], refs[17:34], refs[34:51], refs[51], refs[52]
    loads = [pltpu.make_async_copy(ins[i], bufs[i], sin.at[i]) for i in range(17)]
    stores = [pltpu.make_async_copy(bufs[i], outs[i], sout.at[i]) for i in range(17)]
    factor = jnp.minimum(1.0, clip_limit / (norm[...] + 1e-06))
    width = FF // shards
    order = (2, 3, 0, 1, 4)
    for number in order:
        for i in range(3 * number, 3 * number + 3):
            loads[i].start()
    for i in (15, 16):
        loads[i].start()

    def part(number, rows, lanes, gradient, rate=matrix_rate, decay=decay_rate):
        trio = bufs[3 * number : 3 * number + 3]
        new = adamw(*(ref[rows, lanes] for ref in trio), gradient.astype(F32), factor, rate, decay)
        for ref, value in zip((trio[1], trio[2], trio[0]), new):
            ref[rows, lanes] = value

    def expand(rows):
        for j in range(FF // D):
            for s in range(shards):
                f = s * width + j * 128
                part(2, rows, slice(f, f + 128), own[5 + 2 * j, rows, s * 128 : s * 128 + 128])

    def shrink(rows):
        for j in range(FF // D):
            there = pl.ds(pl.multiple_of(j * 128 + rows.start, 16), rows.size)
            part(3, there, slice(None), own[4 + 2 * j, rows])

    def qkv(rows):
        for i in range(3):
            part(0, rows, slice(i * D, i * D + D), own[1 + i, rows])

    def dense(rows):
        part(1, rows, slice(None), own[0, rows])

    def vectors(rows):
        part(4, slice(None), slice(None), gtable[:VROWS], vector_rate, 0.0)

    for number in order:
        for i in range(3 * number, 3 * number + 3):
            loads[i].wait()
        work = (qkv, dense, expand, shrink, vectors)[number]
        if number == 4:
            work(None)
        else:

            def some(i, carry, work=work):
                work(pl.ds(pl.multiple_of(i * 16, 16), 16))
                return carry

            lax.fori_loop(0, 8, some, 0)
        for i in range(3 * number, 3 * number + 3):
            stores[i].start()
    for i in (15, 16):
        loads[i].wait()
        stores[i].start()
    for store in stores:
        store.wait()


def update_all(norm, own, gtable, states, passed, shards):
    arrays = states + passed
    anywhere = [pl.BlockSpec(memory_space=pl.ANY)] * len(arrays)
    inside = [pl.BlockSpec(memory_space=pltpu.VMEM)] * 3

    def kernel(*refs):
        update_kernel(shards, *refs)

    new = pl.pallas_call(
        kernel,
        out_shape=tuple(jax.ShapeDtypeStruct(a.shape, a.dtype) for a in arrays),
        in_specs=inside + anywhere,
        out_specs=tuple(anywhere),
        scratch_shapes=[pltpu.VMEM(a.shape, a.dtype) for a in arrays]
        + [pltpu.SemaphoreType.DMA((len(arrays),)), pltpu.SemaphoreType.DMA((len(arrays),))],
        compiler_params=pltpu.CompilerParams(vmem_limit_bytes=56 * MIB),
        name="update",
    )(norm, own, gtable, *arrays)
    ordered = [new[3 * i + k] for i in range(5) for k in (1, 2, 0)]
    return ordered + list(new[15:])


def body(
    tokens,
    doc_lengths,
    cotangent,
    qkv_weight,
    qkv_firsts,
    qkv_seconds,
    dense_weight,
    dense_firsts,
    dense_seconds,
    expand_weight,
    expand_firsts,
    expand_seconds,
    shrink_weight,
    shrink_firsts,
    shrink_seconds,
    vectors,
    vec_firsts,
    vec_seconds,
    *,
    shards,
    reps,
):
    nz = shards // 2
    vec_own = jnp.pad(vectors.astype(BF).T, ((0, VPAD - VROWS), (0, 0)))
    full, table, ht, act = front(
        doc_lengths, tokens, cotangent, qkv_weight, dense_weight, vec_own, expand_weight, shrink_weight, nz
    )
    output, grad_in, owned, gtable, norm = back(
        tokens, cotangent, ht, table, act, full.reshape(UNITS, D, D), nz, reps
    )
    owned = owned.reshape(UNITS, 128, D)
    if reps != 4:
        quads = [[4 * i + j for i in range(reps // 4)] for j in range(4)]
        owned = lax.psum(owned, "rep", axis_index_groups=quads)
        gtable, norm = norm_all(gtable, owned, shards, reps)
    states = (
        qkv_weight, qkv_firsts, qkv_seconds,
        dense_weight, dense_firsts, dense_seconds,
        expand_weight, expand_firsts, expand_seconds,
        shrink_weight, shrink_firsts, shrink_seconds,
        vectors.T, vec_firsts.T, vec_seconds.T,
    )
    new = tuple(update_all(norm, owned, gtable, states, (output, grad_in), shards))
    return new[15:] + new[:12] + tuple(vec.T for vec in new[12:15]) + (norm.reshape(1),)


def solution(mesh):
    shards, reps = mesh.shape["shard"], mesh.shape["rep"]
    data, state = P(("rep", "shard"), None), P("shard", None)

    def step(*args):
        return body(*args, shards=shards, reps=reps)

    return jax.shard_map(
        step,
        mesh=mesh,
        in_specs=(data, data, data) + (state,) * 15,
        out_specs=(data, data) + (state,) * 15 + (P(),),
        check_vma=False,
    )
```

```python
import math

import jax
import jax.numpy as jnp
from jax import lax
from jax.experimental import pallas as pl
from jax.experimental.pallas import tpu as pltpu
from jax.sharding import PartitionSpec as P

D = 1024
HEADS = 16
HEAD_DIM = 64
ROTARY = 32
FF = 4096
LEN = 1024
STEP = 10
VROWS = 11
VPAD = 16
UNITS = 12
QB = 256

clip_limit = 1.0
matrix_rate = 0.05
vector_rate = 0.8
decay_rate = 0.1

BF = jnp.bfloat16
F32 = jnp.float32
MIB = 1 << 20


def dot(a, b, ca, cb):
    return lax.dot_general(a, b, (((ca,), (cb,)), ((), ())), preferred_element_type=F32)


class Place:
    def __init__(self, nz):
        self.nz = nz
        self.r = lax.axis_index("rep")
        self.s = lax.axis_index("shard")
        self.z, self.x = self.s // 2, self.s % 2
        self.c = self.r % 2
        self.y = (self.r // 2) % 2
        self.p = 2 * self.c + self.y

    def dev(self, r, s):
        return {"rep": r, "shard": s}

    def zpeer(self, k):
        return self.dev(self.r, ((self.z + k) % self.nz) * 2 + self.x)

    @property
    def xpeer(self):
        return self.dev(self.r, self.z * 2 + 1 - self.x)

    @property
    def ypeer(self):
        return self.dev(self.r + 2 - 4 * self.y, self.s)

    @property
    def cpeer(self):
        return self.dev(self.r + 1 - 2 * self.c, self.s)

    @property
    def diag(self):
        return self.dev(self.r + 2 - 4 * self.y + 1 - 2 * self.c, self.s)

    def swap(self, first):
        on_x = self.c == (0 if first else 1)
        return self.dev(
            jnp.where(on_x, self.r, self.r + 2 - 4 * self.y),
            jnp.where(on_x, self.z * 2 + 1 - self.x, self.s),
        )


def hail(peers):
    barrier = pltpu.get_barrier_semaphore()
    for peer in peers:
        pl.semaphore_signal(barrier, inc=1, device_id=peer, device_id_type=pl.DeviceIdType.MESH)


def hear(peers):
    pl.semaphore_wait(pltpu.get_barrier_semaphore(), len(peers))


def greet(peers):
    hail(peers)
    hear(peers)


def remote(src, dst, send, recv, peer):
    return pltpu.make_async_remote_copy(
        src_ref=src,
        dst_ref=dst,
        send_sem=send,
        recv_sem=recv,
        device_id=peer,
        device_id_type=pl.DeviceIdType.MESH,
    )


class Gather:
    STAGES = 5

    def __init__(self, at, own, full, u0, n, lane, width, send, recv, job):
        self.at, self.own, self.full = at, own, full
        self.us, self.lanes = pl.ds(u0, n), pl.ds(lane, width)
        self.send, self.recv, self.job = send, recv, job

    def rows(self, count):
        at = self.at
        return pl.ds(at.c * 64 + at.y * 32, 32) if count == 32 else pl.ds(at.c * 64, 64)

    def part(self, z, x, rows):
        return self.full.at[self.us, z, x, rows, self.lanes]

    def copy(self, i, src, dst, peer):
        return remote(src, dst, self.send.at[self.job, i], self.recv.at[self.job, i], peer)

    def all_of(self, i):
        every = slice(None)
        z, x, count = ((pl.ds(0, self.at.nz - 1), 0, 32), (every, 0, 32), (every, every, 32), (every, every, 64))[i]
        ref = self.part(z, x, pl.ds(0, count))
        return self.copy(i, ref, ref, self.at.cpeer)

    def stage0(self):
        at = self.at
        src = self.own.at[self.us, self.rows(32), self.lanes]
        for k in range(1, at.nz):
            self.copy(0, src, self.part(at.z, at.x, self.rows(32)), at.zpeer(k)).start()

    def stage1(self):
        self.all_of(0).wait_recv()
        ref = self.part(slice(None), self.at.x, self.rows(32))
        self.copy(1, ref, ref, self.at.swap(True)).start()

    def stage2(self):
        at = self.at
        self.all_of(1).wait_recv()
        along_y = self.part(slice(None), slice(None), self.rows(32))
        along_x = self.part(slice(None), at.x, self.rows(64))
        pl.when(at.c == 0)(lambda: self.copy(2, along_y, along_y, at.ypeer).start())
        pl.when(at.c == 1)(lambda: self.copy(2, along_x, along_x, at.xpeer).start())

    def stage3(self):
        self.all_of(2).wait_recv()
        ref = self.part(slice(None), slice(None), self.rows(64))
        self.copy(3, ref, ref, self.at.cpeer).start()

    def stage4(self):
        self.all_of(3).wait_recv()
        for i in range(4):
            self.all_of(i).wait_send()


def rotate_rows(u, cosine, sine):
    top = u[:16] * cosine - u[16:32] * sine
    low = u[16:32] * cosine + u[:16] * sine
    return jnp.concatenate([top, low, u[32:]], axis=0)


def heads_attention(bias, qt, kt, vt, gt, act, dqt, dkt, dvt, pause):
    def scores(head, number):
        q0 = number * QB
        k0 = max(0, number - 2) * QB
        span = q0 + QB - k0
        rows = slice(64 * head, 64 * head + 64)
        q, g = qt[rows, q0 : q0 + QB], gt[rows, q0 : q0 + QB]
        k, v = kt[rows, k0 : k0 + span], vt[rows, k0 : k0 + span]
        return q, g, k, v, dot(k, q, 0, 0) + bias[number, :span], dot(v, g, 0, 0)

    def weigh(head, number, q, g, k, v, s, dp):
        rows = slice(64 * head, 64 * head + 64)
        e = jnp.exp(s - jnp.max(s, axis=0, keepdims=True))
        p = e * (1.0 / jnp.sum(e, axis=0, keepdims=True))
        pb = p.astype(BF)
        o = dot(v, pb, 1, 0)
        inner = jnp.sum(o * g.astype(F32), axis=0, keepdims=True)
        ds = (p * (dp - inner)).astype(BF)
        act[0, rows, number * QB : number * QB + QB] = o.astype(BF)
        return q, g, k, pb, ds

    def spread(head, number, q, g, k, pb, ds):
        q0 = number * QB
        k0 = max(0, number - 2) * QB
        old = q0 - k0
        rows = slice(64 * head, 64 * head + 64)
        dqt[rows, q0 : q0 + QB] = dot(k, ds, 1, 0)
        dk = dot(q, ds, 1, 1)
        dv = dot(g, pb, 1, 1)
        if old:
            dkt[rows, k0:q0] += dk[:, :old]
            dvt[rows, k0:q0] += dv[:, :old]
        dkt[rows, q0 : q0 + QB] = dk[:, old:]
        dvt[rows, q0 : q0 + QB] = dv[:, old:]

    order = [(head, number) for number in range(LEN // QB) for head in range(4)]
    ready, waiting = scores(*order[0]), None
    for i, (head, number) in enumerate(order):
        following = scores(*order[i + 1]) if i + 1 < len(order) else None
        weighed = weigh(head, number, *ready)
        if waiting is not None:
            spread(*waiting)
        waiting, ready = (head, number, *weighed), following
        if i % 4 == 3:
            pause(i // 4)
    spread(*waiting)


JOBS = UNITS + 1
READY = 6
LAGS = (0, 1, 2, 4, 5)


def run_stage(gather, stage):
    getattr(gather, f"stage{stage}")()


def front_kernel(
    nz,
    lengths, tokens_hbm, dy_hbm, wqkv, wd, vec, wexpand, wshrink,
    full, table, ht_hbm, act_hbm, grads_hbm,
    tokens, dy, ht, act, gqkv, gdense, own, expand_f, shrink_f, wd_v, wq_v, bias, cosine, sine, qt, kt, vt, gt, dqf, dkf, dvf,
    send, recv, vsend, vrecv, lsem,
):
    at = Place(nz)
    shards = 2 * nz
    others = [at.dev(at.r, (at.s + k) % shards) for k in range(1, shards)]
    hail(others + [at.ypeer, at.cpeer])
    load_expand = pltpu.make_async_copy(wexpand, expand_f, lsem.at[0])
    load_shrink = pltpu.make_async_copy(wshrink, shrink_f, lsem.at[1])
    load_tokens = pltpu.make_async_copy(tokens_hbm, tokens, lsem.at[7])
    load_dy = pltpu.make_async_copy(dy_hbm, dy, lsem.at[8])
    store_ht = pltpu.make_async_copy(ht, ht_hbm, lsem.at[9])
    for load in (load_tokens, load_dy, load_expand, load_shrink):
        load.start()
    own[0] = wd[...].astype(BF)
    for i in range(3):
        own[1 + i] = wqkv[:, i * D : i * D + D].astype(BF)
    hear(others + [at.ypeer, at.cpeer])

    def lanes(i):
        return pl.ds(pl.multiple_of(i * 128, 128), 128)

    vcopies = [
        remote(vec, table.at[:, lanes(at.s)], vsend.at[k], vrecv.at[k], peer)
        for k, peer in enumerate(others)
    ]
    for copy in vcopies:
        copy.start()
    table[:, lanes(at.s)] = vec[...]
    mine = pl.ds(at.p * 32, 32)
    local_a = pltpu.make_async_copy(
        own.at[0:4, mine], full.at[0:4, at.z, at.x, mine], lsem.at[2]
    )
    local_a.start()
    local_f = pltpu.make_async_copy(
        own.at[4:UNITS, mine], full.at[4:UNITS, at.z, at.x, mine], lsem.at[3]
    )

    def cast_rest():
        load_expand.wait()
        load_shrink.wait()
        width = FF // shards
        for j in range(FF // D):
            own[4 + 2 * j] = shrink_f[j * 128 : j * 128 + 128].astype(BF)
            for b in range(shards):
                own[5 + 2 * j, :, b * 128 : b * 128 + 128] = expand_f[
                    :, b * width + j * 128 : b * width + j * 128 + 128
                ].astype(BF)
        local_f.start()

    def tables():
        place = lax.broadcasted_iota(jnp.int32, (1, LEN), 1)
        start = jnp.zeros((1, LEN), jnp.int32)
        end = 0
        for d in range(lengths.shape[1]):
            end = end + lengths[0, d]
            start = start + jnp.where(place >= end, lengths[0, d], 0)
        m = lax.broadcasted_iota(jnp.int32, (ROTARY // 2, LEN), 0).astype(F32)
        frequency = jnp.exp(m * (-2.0 * math.log(10000.0) / ROTARY))
        angle = (place - start).astype(F32) * frequency
        cosine[...] = jnp.cos(angle)
        sine[...] = jnp.sin(angle)
        for number in range(LEN // QB):
            q0 = number * QB
            k0 = max(0, number - 2) * QB
            span = q0 + QB - k0
            j = k0 + lax.broadcasted_iota(jnp.int32, (span, QB), 0)
            i = q0 + lax.broadcasted_iota(jnp.int32, (span, QB), 1)
            allowed = (j >= start[:, q0 : q0 + QB]) & (j <= i)
            bias[number, :span] = jnp.where(allowed, 0.0, -1e30)

    def wait_vec():
        for k, copy in enumerate(vcopies):
            came = (at.s + shards - (k + 1)) % shards
            remote(vec, table.at[:, lanes(came)], vsend.at[k], vrecv.at[k], others[k]).wait_recv()
            copy.wait_send()

    def norm_rows(i):
        rows = pl.ds(pl.multiple_of(i * 256, 256), 256)
        x = tokens[rows].astype(F32)
        centered = x - jnp.mean(x, axis=1, keepdims=True)
        scaled = centered * lax.rsqrt(jnp.mean(centered * centered, axis=1, keepdims=True) + 1e-05)
        h = scaled * table[0:1].astype(F32) + table[1:2].astype(F32)
        ht[:, rows] = h.astype(BF).T

    def part(job, stage):
        args = (send, recv, job)
        if isinstance(job, int):
            if job == 1:
                gather = Gather(at, own, full, 0, 1, 0, D, *args)
            elif job < 5:
                gather = Gather(at, own, full, 1, 3, 256 * max(0, job - 1), 256, *args)
            else:
                gather = Gather(at, own, full, job - 1, 1, 0, D, *args)
            run_stage(gather, stage)
            return
        lane = pl.multiple_of((job - 1) * 256, 256)
        pl.when((job >= 2) & (job < 5))(
            lambda: run_stage(Gather(at, own, full, 1, 3, lane, 256, *args), stage)
        )
        pl.when((job >= 5) & (job < JOBS))(
            lambda: run_stage(Gather(at, own, full, job - 1, 1, 0, D, *args), stage)
        )

    def load_quad(quad):
        lane = quad * 256 if isinstance(quad, int) else pl.multiple_of(quad * 256, 256)
        src = full.at[pl.ds(1, 3), :, :, :, pl.ds(lane, 256)]
        return pltpu.make_async_copy(src, wq_v.at[quad % 2], lsem.at[4 + quad % 2])

    load_dense = pltpu.make_async_copy(full.at[0], wd_v, lsem.at[6])
    side = {
        0: (tables,),
        1: (wait_vec, load_tokens.wait, lambda: norm_rows(0)),
        2: (lambda: norm_rows(1), lambda: norm_rows(2)),
        3: (lambda: norm_rows(3), store_ht.start),
        4: (cast_rest,),
    }
    for step in range(READY):
        for stage in range(Gather.STAGES):
            if 0 <= step - stage < 2:
                if step == 1 and stage == 1:
                    local_a.wait()
                part(step - stage, stage)
            if step - LAGS[stage] >= 2:
                part(step - LAGS[stage], stage)
        for what in side.get(step, ()):
            what()
        if step == 4:
            load_quad(0).start()
    load_dense.start()
    local_f.wait()

    def prepare(quad):
        cols = pl.ds(pl.multiple_of(quad * 256, 256), 256)
        load_quad(quad).wait()
        pl.when(quad == 0)(load_dense.wait)
        pl.when(quad == 0)(load_dy.wait)
        for part, dst in enumerate((qt, kt, vt)):
            w = wq_v[quad % 2, part].reshape(D, 256)
            u = dot(w, ht[...], 0, 0)
            ones = jnp.ones((1, 128), BF)
            b = dot(table[2 + part : 3 + part, cols], ones, 0, 0)[:, :1]
            u = u + b
            if part == 2:
                dst[...] = u.astype(BF)
                continue
            for head in range(4):
                turned = rotate_rows(u[head * 64 : head * 64 + 64], cosine[...], sine[...])
                if part == 0:
                    turned = turned * (1.0 / math.sqrt(HEAD_DIM))
                dst[head * 64 : head * 64 + 64] = turned.astype(BF)
        for half in range(2):
            w = wd_v[quad, half]
            gt[half * 128 : half * 128 + 128] = dot(w, dy[...], 1, 1).astype(BF)

    def store_act(quad):
        rows = pl.ds(pl.multiple_of(quad * 256, 256), 256)
        return pltpu.make_async_copy(act.at[quad % 2], act_hbm.at[:, rows], lsem.at[10 + quad % 2])

    def store_grads(quad):
        part = pl.ds(pl.multiple_of(quad * 256, 256), 256)
        slot = quad % 2
        return (
            pltpu.make_async_copy(
                gqkv.at[slot], grads_hbm.at[pl.ds(1, 3), :, part], lsem.at[12 + slot]
            ),
            pltpu.make_async_copy(gdense.at[slot], grads_hbm.at[0, part], lsem.at[14 + slot]),
        )

    def stored(quad):
        store_act(quad).wait()
        for copy in store_grads(quad):
            copy.wait()

    def one_quad(quad, carry):
        prepare(quad)
        pl.when(quad >= 2)(lambda: stored(quad - 2))
        here = act.at[quad % 2]

        def pause(number):
            if number != 1:
                for stage, lag in enumerate(LAGS):
                    part(READY + 3 * quad + max(0, number - 1) - lag, stage)

            if number == 2:
                pl.when(quad < 3)(lambda: load_quad(quad + 1).start())

        heads_attention(bias, qt, kt, vt, gt, here, dqf, dkf, dvf, pause)
        for head in range(4):
            rows = slice(64 * head, 64 * head + 64)
            back = rotate_rows(dqf[rows], cosine[...], -sine[...]) * (1.0 / math.sqrt(HEAD_DIM))
            here[1, rows] = back.astype(BF)
            here[2, rows] = rotate_rows(dkf[rows], cosine[...], -sine[...]).astype(BF)
            here[3, rows] = dvf[rows].astype(BF)
        store_act(quad).start()
        for i in range(3):
            gqkv[quad % 2, i] = dot(ht[...], here[1 + i], 1, 1).astype(BF)
        gdense[quad % 2] = dot(here[0], dy[...], 1, 0).astype(BF)
        for copy in store_grads(quad):
            copy.start()
        return carry

    lax.fori_loop(0, 4, one_quad, 0)
    for quad in (2, 3):
        stored(quad)
    store_ht.wait()


def front(lengths, tokens, dy, wqkv, wd, vec, wexpand, wshrink, nz):
    shards = 2 * nz
    anywhere = pl.BlockSpec(memory_space=pl.ANY)
    inside = pl.BlockSpec(memory_space=pltpu.VMEM)

    def kernel(*refs):
        front_kernel(nz, *refs)

    return pl.pallas_call(
        kernel,
        out_shape=(
            jax.ShapeDtypeStruct((UNITS, nz, 2, 128, D), BF),
            jax.ShapeDtypeStruct((VPAD, D), BF),
            jax.ShapeDtypeStruct((D, LEN), BF),
            jax.ShapeDtypeStruct((4, D, LEN), BF),
            jax.ShapeDtypeStruct((4, D, D), BF),
        ),
        in_specs=[
            pl.BlockSpec(memory_space=pltpu.SMEM),
            anywhere,
            anywhere,
            inside,
            inside,
            inside,
            anywhere,
            anywhere,
        ],
        out_specs=(anywhere, inside, anywhere, anywhere, anywhere),
        scratch_shapes=[
            pltpu.VMEM((LEN, D), BF),
            pltpu.VMEM((LEN, D), BF),
            pltpu.VMEM((D, LEN), BF),
            pltpu.VMEM((2, 4, 256, LEN), BF),
            pltpu.VMEM((2, 3, D, 256), BF),
            pltpu.VMEM((2, 256, D), BF),
            pltpu.VMEM((UNITS, 128, D), BF),
            pltpu.VMEM(wexpand.shape, F32),
            pltpu.VMEM(wshrink.shape, F32),
            pltpu.VMEM((nz, 2, 128, D), BF),
            pltpu.VMEM((2, 3, nz, 2, 128, 256), BF),
            pltpu.VMEM((LEN // QB, 3 * QB, QB), F32),
            pltpu.VMEM((ROTARY // 2, LEN), F32),
            pltpu.VMEM((ROTARY // 2, LEN), F32),
            pltpu.VMEM((256, LEN), BF),
            pltpu.VMEM((256, LEN), BF),
            pltpu.VMEM((256, LEN), BF),
            pltpu.VMEM((256, LEN), BF),
            pltpu.VMEM((256, LEN), F32),
            pltpu.VMEM((256, LEN), F32),
            pltpu.VMEM((256, LEN), F32),
            pltpu.SemaphoreType.DMA((JOBS, 4)),
            pltpu.SemaphoreType.DMA((JOBS, 4)),
            pltpu.SemaphoreType.DMA((shards - 1,)),
            pltpu.SemaphoreType.DMA((shards - 1,)),
            pltpu.SemaphoreType.DMA((16,)),
        ],
        compiler_params=pltpu.CompilerParams(
            collective_id=0, has_side_effects=True, vmem_limit_bytes=58 * MIB
        ),
        name="front",
    )(lengths, tokens, dy, wqkv, wd, vec, wexpand, wshrink)


RC, RB = 3, 6


class Reduce:
    def __init__(self, at, grads, rc, rb, ra, rz, out, send, recv):
        self.at = at
        self.grads, self.rc, self.rb, self.ra, self.rz, self.out = grads, rc, rb, ra, rz, out
        self.send, self.recv = send, recv

    SEMS = 6

    def copy(self, u, i, src, dst, peer):
        send = self.send.at[u, i] if i < 3 else self.send.at[UNITS, i]
        return remote(src, dst, send, self.recv.at[u, i], peer)

    def finish(self):
        pieces = self.out.at[:, pl.ds(0, 1)], self.out.at[:, pl.ds(0, 2)]
        for i, ref in enumerate((self.rz,) + pieces):
            remote(ref, ref, self.send.at[UNITS, 3 + i], self.recv.at[0, 3 + i], self.at.cpeer).wait_send()

    def c(self, u):
        at = self.at
        return self.copy(u, 0, self.grads.at[u % 2, :, :, 1 - at.c], self.rc.at[u % RC], at.cpeer)

    def on_x(self, u):
        return (self.at.c == 1) | (u % 4 == 3)

    def b(self, u, on_x):
        at = self.at
        rc = self.rc.at[u % RC]
        src = rc.at[:, 1 - at.x] if on_x else rc.at[:, :, 1 - at.y]
        return self.copy(u, 1, src, self.rb.at[u % RB], at.xpeer if on_x else at.ypeer)

    def a(self, u, on_x):
        at = self.at
        src = self.rb.at[u % RB, :, 1 - (at.y if on_x else at.x)]
        return self.copy(u, 2, src, self.ra.at[u], at.ypeer if on_x else at.xpeer)

    def z(self, u, k):
        at = self.at
        src = self.ra.at[u, (at.z + k) % at.nz]
        return self.copy(u, 3, src, self.rz.at[u, k - 1], at.zpeer(k))

    def f(self, u):
        ref = self.out.at[u, self.at.p]
        return self.copy(u, 4, ref, ref, self.at.ypeer)

    def f_in(self, u):
        ref = self.out.at[u, 2 * self.at.c + 1 - self.at.y]
        return self.copy(u, 4, ref, ref, self.at.ypeer)

    def g(self, u):
        ref = self.out.at[u, pl.ds(2 * self.at.c, 2)]
        return self.copy(u, 5, ref, ref, self.at.cpeer)

    def g_in(self, u):
        ref = self.out.at[u, pl.ds(2 - 2 * self.at.c, 2)]
        return self.copy(u, 5, ref, ref, self.at.cpeer)

    def either(self, u, what):
        on_x = self.on_x(u)
        pl.when(on_x)(lambda: what(True))
        pl.when(jnp.logical_not(on_x))(lambda: what(False))

    def phase0(self, u):
        self.c(u).start()

    def phase1(self, u):
        at = self.at
        self.c(u).wait_recv()
        add_into(self.rc.at[u % RC], self.grads.at[u % 2, :, :, at.c])
        self.c(u).wait_send()
        self.either(u, lambda on_x: self.b(u, on_x).start())

    def phase2(self, u):
        at = self.at
        rc, rb = self.rc.at[u % RC], self.rb.at[u % RB]
        self.b(u, True).wait_recv()

        def add(on_x):
            add_into(rb, rc.at[:, at.x] if on_x else rc.at[:, :, at.y])
            self.a(u, on_x).start()

        self.either(u, add)
        self.b(u, True).wait_send()

    def phase3(self, u):
        at = self.at
        self.a(u, True).wait_recv()
        turn = jnp.where(self.on_x(u), at.y, at.x)
        add_into(self.ra.at[u], self.rb.at[u % RB, :, turn])
        for k in range(1, at.nz):
            self.z(u, k).start()
        self.a(u, True).wait_send()

    def phase4(self, u):
        at = self.at
        total = self.ra[u, at.z].astype(F32)
        self.copy(u, 3, self.rz.at[u], self.rz.at[u], at.cpeer).wait_recv()
        for k in range(1, at.nz):
            total += self.rz[u, k - 1].astype(F32)
        self.out[u, at.p] = total.astype(BF)
        self.f(u).start()

    def phase5(self, u):
        self.f_in(u).wait_recv()
        self.g(u).start()

    def phase6(self, u):
        self.g_in(u).wait_recv()


PHASES = 7
OFFSETS = (0, 1, 2, 3, 4, 5, 6)


def add_into(dst, src):
    dst[...] = dst[...] + src[...]


class VecSum:
    def __init__(self, shards, reps, gvec, v1, v2, sq, send, recv):
        self.shards, self.reps = shards, reps
        self.r, self.s = lax.axis_index("rep"), lax.axis_index("shard")
        self.row = [{"rep": self.r, "shard": (self.s + k) % shards} for k in range(1, shards)]
        self.col = [{"rep": (self.r + k) % reps, "shard": self.s} for k in range(1, reps)]
        self.gvec, self.v1, self.v2, self.sq = gvec, v1, v2, sq
        self.send, self.recv = send, recv

    @staticmethod
    def sems(shards, reps):
        return 2 * (shards - 1) + reps - 1

    def lanes(self, i):
        return pl.ds(pl.multiple_of(i * 128, 128), 128)

    def copy(self, i, src, dst, peer):
        return remote(src, dst, self.send.at[i], self.recv.at[i], peer)

    def over_shards(self, k):
        src = self.gvec.at[:, self.lanes((self.s + k) % self.shards)]
        return self.copy(k - 1, src, self.v1.at[self.s], self.row[k - 1])

    def over_reps(self, k):
        ref = self.v2.at[self.r]
        return self.copy(self.shards + k - 2, ref, ref, self.col[k - 1])

    def squares(self, k):
        ref = self.sq.at[self.s]
        return self.copy(self.shards + self.reps + k - 3, ref, ref, self.row[k - 1])

    def total(self, ref, count):
        every = ref[0]
        for i in range(1, count):
            every += ref[i]
        return every

    def stage0(self):
        for k in range(1, self.shards):
            self.over_shards(k).start()
        self.v1[self.s] = self.gvec[:, self.lanes(self.s)]

    def stage1(self):
        for k in range(1, self.shards):
            dst = self.v1.at[(self.s + self.shards - k) % self.shards]
            self.copy(k - 1, dst, dst, self.row[k - 1]).wait_recv()
            self.over_shards(k).wait_send()
        self.v2[self.r] = self.total(self.v1, self.shards)
        for k in range(1, self.reps):
            self.over_reps(k).start()

    def stage2(self):
        for k in range(1, self.reps):
            dst = self.v2.at[(self.r + self.reps - k) % self.reps]
            self.copy(self.shards + k - 2, dst, dst, self.col[k - 1]).wait_recv()
            self.over_reps(k).wait_send()
        return self.total(self.v2, self.reps)

    def norm(self, wide, table):
        part = table[:8] * table[:8] + table[8:] * table[8:]
        for i in range(D // 128):
            part += wide[:, i * 128 : i * 128 + 128]
        self.sq[self.s] = part
        for k in range(1, self.shards):
            self.squares(k).start()
        for k in range(1, self.shards):
            i = self.shards + self.reps + k - 3
            dst = self.sq.at[(self.s + self.shards - k) % self.shards]
            self.copy(i, dst, dst, self.row[k - 1]).wait_recv()
            self.squares(k).wait_send()
        return jnp.sqrt(jnp.sum(self.total(self.sq, self.shards), keepdims=True))


def fold_squares(block):
    g = block.astype(F32)
    return jnp.sum((g * g).reshape(-1, 8, D), axis=0)


WIDE = 512


def cols(n, width=WIDE):
    return pl.ds(pl.multiple_of(n * width, width), width)


def tiles(run):
    def one(n, carry):
        run(n)
        return carry

    lax.fori_loop(0, D // WIDE, one, 0)


def back_kernel(
    nz, reps,
    tokens, dy_hbm, ht_hbm, table, act, full, ready,
    out_hbm, grad_hbm, owned, gtable, norm,
    dy, ht, grad_in, wb, grads, rc, rb, ra, rz, gelu, dact, acc, b1, gb1, gv, wide, v1, v2, sq,
    send, recv, vsend, vrecv, wsem, osem, gsem,
):
    at = Place(nz)
    shards = 2 * nz
    fused = reps == 4
    width = FF // shards

    def load(slot, first, second):
        for i, src in enumerate((first, second)):
            pltpu.make_async_copy(src, wb.at[slot, i], wsem.at[slot, i]).start()

    def loaded(slot):
        for i in range(2):
            pltpu.make_async_copy(full.at[0], wb.at[slot, i], wsem.at[slot, i]).wait()

    def load_mlp(j):
        load((j + 2) % 3, full.at[4 + 2 * j], full.at[5 + 2 * j])

    load_dy = pltpu.make_async_copy(dy_hbm, dy, osem.at[2])
    load_ht = pltpu.make_async_copy(ht_hbm, ht, osem.at[3])
    vecs = VecSum(shards, reps, gv, v1, v2, sq, vsend, vrecv)
    peers = vecs.row + [at.ypeer, at.cpeer, at.diag]
    hail(peers)

    def load_grad(u):
        return pltpu.make_async_copy(ready.at[u], grads.at[u % 2], gsem.at[u % 2])

    load_grad(0).start()
    load_grad(1).start()
    load_dy.start()
    load_ht.start()
    for j in range(3):
        load_mlp(j)
    out = wb.at[0, 1]
    out_copy = pltpu.make_async_copy(out, out_hbm, osem.at[0])
    grad_copy = pltpu.make_async_copy(grad_in, grad_hbm, osem.at[1])
    red = Reduce(at, grads, rc, rb, ra, rz, owned, send, recv)
    hear(peers)

    def prepare():
        gv[...] = jnp.zeros((VPAD, D), F32)
        wide[...] = jnp.zeros((8, D), F32)
        grad_in[...] = jnp.zeros((LEN, D), F32)
        acc[...] = jnp.zeros((LEN, D), F32)
        for j in range(FF // D):
            for s in range(shards):
                f = s * width + j * 128
                b1[j : j + 1, s * 128 : s * 128 + 128] = table[
                    6 + f // D : 7 + f // D, f % D : f % D + 128
                ].astype(F32)

    def write(u, n, value):
        grads[u % 2, :, :, :, :, :, cols(n)] = value.astype(BF).reshape(nz, 2, 2, 2, 32, WIDE)

    def activate(j, half):
        slot = (j + 2) % 3
        parts = [pl.ds(pl.multiple_of(half * 512 + n * 256, 256), 256) for n in range(2)]
        products = []
        for part in parts:
            a = dot(ht[...], wb[slot, 1, :, part], 0, 0)
            products.append((a, dot(dy[...], wb[slot, 0, part, :], 1, 1)))
        for part, (a, dg) in zip(parts, products):
            a = a + b1[pl.ds(j, 1), part]
            square = a * a
            t = jnp.tanh(a * (math.sqrt(2.0 / math.pi) + (math.sqrt(2.0 / math.pi) * 0.044715) * square))
            gate = 0.5 + 0.5 * t
            gelu[j % 2, :, part] = (a * gate).astype(BF)
            slope = gate + a * (1.0 - t * t) * (
                0.5 * math.sqrt(2.0 / math.pi) + (1.5 * 0.044715 * math.sqrt(2.0 / math.pi)) * square
            )
            da = (dg * slope).astype(BF)
            dact[j % 2, :, part] = da
            gb1[pl.ds(j, 1), part] = jnp.sum(da.astype(F32), axis=0, keepdims=True)

    def finish():
        gain = table[0:1].astype(F32)
        shift = table[5:6].astype(F32) + table[10:11].astype(F32)

        def rows_of(i, carry):
            rows = pl.ds(pl.multiple_of(i * 128, 128), 128)
            x = wb[0, 0, rows].astype(F32)
            out[rows] = (x + acc[rows] + shift).astype(BF)
            centered = x - jnp.mean(x, axis=1, keepdims=True)
            rstd = lax.rsqrt(jnp.mean(centered * centered, axis=1, keepdims=True) + 1e-05)
            n = centered * rstd
            dh = grad_in[rows]
            back = dy[rows].astype(F32)
            e = dh * gain
            grad_in[rows] = back + rstd * (
                e
                - jnp.mean(e, axis=1, keepdims=True)
                - n * jnp.mean(e * n, axis=1, keepdims=True)
            )
            gv[0:1] += jnp.sum(dh * n, axis=0, keepdims=True)
            gv[1:2] += jnp.sum(dh, axis=0, keepdims=True)
            gv[5:6] += jnp.sum(back, axis=0, keepdims=True)
            return carry

        lax.fori_loop(0, LEN // 128, rows_of, 0)
        gv[10:11] = gv[5:6]
        for j in range(FF // D):
            for s in range(shards):
                f = s * width + j * 128
                gv[6 + f // D : 7 + f // D, f % D : f % D + 128] = gb1[
                    j : j + 1, s * 128 : s * 128 + 128
                ]

    def tick(t, carry):
        for number in range(1, PHASES):
            u = t - OFFSETS[number]

            def phase(u=u, number=number):
                getattr(red, f"phase{number}")(u)
                if number == PHASES - 1 and fused:
                    wide[...] += fold_squares(owned[u])

            pl.when((u >= 0) & (u < UNITS))(phase)

        even, odd = t % 2 == 0, t % 2 == 1
        shrink, expand = (t >= 4) & (t < UNITS) & even, (t >= 4) & (t < UNITS) & odd
        again = (t >= 8) & (t < UNITS)
        j = (t - 4) // 2

        pl.when((t == 1) | (t == 2))(lambda: load_grad(t + 1).start())
        pl.when(t == 6)(lambda: load_mlp(3))
        pl.when(again)(lambda: load(0, act.at[t - 8], full.at[t - 8]))
        inputs = pltpu.make_async_copy(tokens, wb.at[0, 0], wsem.at[0, 0])
        pl.when(t == 12)(lambda: inputs.start())

        pl.when(t < 4)(lambda: load_grad(t).wait())
        pl.when(shrink)(
            lambda: tiles(lambda n: write(t, n, dot(gelu[j % 2], dy[:, cols(n)], 0, 0)))
        )
        pl.when(expand)(
            lambda: tiles(
                lambda n: write(t, n, dot(ht[...], dact[j % 2, :, cols(n)], 1, 0))
            )
        )
        pl.when(t < UNITS)(lambda: red.phase0(t))
        pl.when(t == 0)(prepare)

        @pl.when(t == 1)
        def _():
            load_dy.wait()
            load_ht.wait()
            loaded(2)

        @pl.when(shrink)
        def _():
            def tile(n):
                acc[:, cols(n)] += dot(gelu[j % 2], wb[(j + 2) % 3, 0, :, cols(n)], 1, 0)

            tiles(tile)

        @pl.when(expand)
        def _():
            def tile(n):
                grad_in[:, cols(n)] += dot(
                    dact[j % 2], wb[(j + 2) % 3, 1, cols(n), :], 1, 1
                )

            tiles(tile)

        pl.when((t == 3) | (t == 5) | (t == 7))(lambda: loaded((t // 2 + 2) % 3))
        pl.when((t >= 1) & (t < 9))(lambda: activate((t - 1) // 2, 1 - t % 2))

        pl.when(again)(lambda: loaded(0))

        @pl.when(t == 8)
        def _():
            def tile(n):
                acc[:, cols(n)] += dot(wb[0, 0], wb[0, 1, :, cols(n)], 0, 0)

            tiles(tile)

        @pl.when(again & (t > 8))
        def _():
            ones = jnp.ones((8, LEN), BF)

            def tile(n):
                grad_in[:, cols(n)] += dot(wb[0, 0], wb[0, 1, cols(n), :], 0, 1)
                gv[pl.ds(t - 7, 1), cols(n)] = dot(ones, wb[0, 0, cols(n), :], 1, 1)[:1]

            tiles(tile)

        @pl.when(t == UNITS + 1)
        def _():
            inputs.wait()
            finish()
            out_copy.start()
            grad_copy.start()

        if fused:
            pl.when(t == UNITS + 2)(vecs.stage0)
            pl.when(t == UNITS + 3)(vecs.stage1)

            @pl.when(t == UNITS + 4)
            def _():
                gtable[...] = vecs.stage2()

        return carry

    lax.fori_loop(0, UNITS + OFFSETS[-1], tick, 0)
    red.finish()
    out_copy.wait()
    grad_copy.wait()
    if fused:
        norm[...] = vecs.norm(wide[...], gtable[...])
    else:
        gtable[...] = gv[...]
        norm[...] = jnp.zeros((1, 1), F32)


def back(tokens, dy, ht, table, act, full, ready, nz, reps):
    shards = 2 * nz
    vcount = VecSum.sems(shards, reps)
    anywhere = pl.BlockSpec(memory_space=pl.ANY)
    inside = pl.BlockSpec(memory_space=pltpu.VMEM)

    def kernel(*refs):
        back_kernel(nz, reps, *refs)

    return pl.pallas_call(
        kernel,
        out_shape=(
            jax.ShapeDtypeStruct((LEN, D), BF),
            jax.ShapeDtypeStruct((LEN, D), F32),
            jax.ShapeDtypeStruct((UNITS, 4, 32, D), BF),
            jax.ShapeDtypeStruct((VPAD, 128 if reps == 4 else D), F32),
            jax.ShapeDtypeStruct((1, 1), F32),
        ),
        in_specs=[anywhere, anywhere, anywhere, inside, anywhere, anywhere, anywhere],
        out_specs=(anywhere, anywhere, inside, inside, inside),
        scratch_shapes=[
            pltpu.VMEM((LEN, D), BF),
            pltpu.VMEM((D, LEN), BF),
            pltpu.VMEM((LEN, D), F32),
            pltpu.VMEM((3, 2, D, D), BF),
            pltpu.VMEM((2, nz, 2, 2, 2, 32, D), BF),
            pltpu.VMEM((RC, nz, 2, 2, 32, D), BF),
            pltpu.VMEM((RB, nz, 2, 32, D), BF),
            pltpu.VMEM((UNITS, nz, 32, D), BF),
            pltpu.VMEM((UNITS, nz - 1, 32, D), BF),
            pltpu.VMEM((2, LEN, D), BF),
            pltpu.VMEM((2, LEN, D), BF),
            pltpu.VMEM((LEN, D), F32),
            pltpu.VMEM((FF // D, D), F32),
            pltpu.VMEM((FF // D, D), F32),
            pltpu.VMEM((VPAD, D), F32),
            pltpu.VMEM((8, D), F32),
            pltpu.VMEM((shards, VPAD, 128), F32),
            pltpu.VMEM((reps, VPAD, 128), F32),
            pltpu.VMEM((shards, 8, 128), F32),
            pltpu.SemaphoreType.DMA((UNITS + 1, Reduce.SEMS)),
            pltpu.SemaphoreType.DMA((UNITS, Reduce.SEMS)),
            pltpu.SemaphoreType.DMA((vcount,)),
            pltpu.SemaphoreType.DMA((vcount,)),
            pltpu.SemaphoreType.DMA((3, 2)),
            pltpu.SemaphoreType.DMA((4,)),
            pltpu.SemaphoreType.DMA((2,)),
        ],
        compiler_params=pltpu.CompilerParams(
            collective_id=1, has_side_effects=True, vmem_limit_bytes=60 * MIB
        ),
        name="back",
    )(tokens, dy, ht, table, act, full, ready)


def norm_kernel(shards, reps, gvec, own, gtable, norm, v1, v2, sq, send, recv):
    vecs = VecSum(shards, reps, gvec, v1, v2, sq, send, recv)
    greet(vecs.row + vecs.col)
    vecs.stage0()
    wide = lax.fori_loop(
        0, own.shape[0], lambda u, acc: acc + fold_squares(own[u]), jnp.zeros((8, D), F32)
    )
    vecs.stage1()
    gtable[...] = vecs.stage2()
    norm[...] = vecs.norm(wide, gtable[...])


def norm_all(gvec, own, shards, reps):
    count = VecSum.sems(shards, reps)

    def kernel(*refs):
        norm_kernel(shards, reps, *refs)

    inside = pl.BlockSpec(memory_space=pltpu.VMEM)
    return pl.pallas_call(
        kernel,
        out_shape=(
            jax.ShapeDtypeStruct((VPAD, 128), F32),
            jax.ShapeDtypeStruct((1, 1), F32),
        ),
        in_specs=[inside, inside],
        out_specs=(inside, inside),
        scratch_shapes=[
            pltpu.VMEM((shards, VPAD, 128), F32),
            pltpu.VMEM((reps, VPAD, 128), F32),
            pltpu.VMEM((shards, 8, 128), F32),
            pltpu.SemaphoreType.DMA((count,)),
            pltpu.SemaphoreType.DMA((count,)),
        ],
        compiler_params=pltpu.CompilerParams(
            collective_id=2, has_side_effects=True, vmem_limit_bytes=56 * MIB
        ),
        name="norm_all",
    )(gvec, own)


def adamw(master, firsts, seconds, gradient, factor, step_rate, decay_amount):
    clipped = gradient * factor
    momentum = 0.9 * firsts + 0.1 * clipped
    variance = 0.95 * seconds + 0.05 * clipped * clipped
    corrected = momentum / (1.0 - 0.9**STEP)
    spread = variance / (1.0 - 0.95**STEP)
    renewed = master - step_rate * (corrected / (jnp.sqrt(spread) + 1e-08) + decay_amount * master)
    return (momentum, variance, renewed)


def update_kernel(shards, norm, own, gtable, *refs):
    ins, outs, bufs, sin, sout = refs[:17], refs[17:34], refs[34:51], refs[51], refs[52]
    loads = [pltpu.make_async_copy(ins[i], bufs[i], sin.at[i]) for i in range(17)]
    stores = [pltpu.make_async_copy(bufs[i], outs[i], sout.at[i]) for i in range(17)]
    factor = jnp.minimum(1.0, clip_limit / (norm[...] + 1e-06))
    width = FF // shards
    order = (2, 3, 0, 1, 4)
    for number in order:
        for i in range(3 * number, 3 * number + 3):
            loads[i].start()
    for i in (15, 16):
        loads[i].start()

    def part(number, rows, lanes, gradient, rate=matrix_rate, decay=decay_rate):
        trio = bufs[3 * number : 3 * number + 3]
        new = adamw(*(ref[rows, lanes] for ref in trio), gradient.astype(F32), factor, rate, decay)
        for ref, value in zip((trio[1], trio[2], trio[0]), new):
            ref[rows, lanes] = value

    def expand(rows):
        for j in range(FF // D):
            for s in range(shards):
                f = s * width + j * 128
                part(2, rows, slice(f, f + 128), own[5 + 2 * j, rows, s * 128 : s * 128 + 128])

    def shrink(rows):
        for j in range(FF // D):
            there = pl.ds(pl.multiple_of(j * 128 + rows.start, 16), rows.size)
            part(3, there, slice(None), own[4 + 2 * j, rows])

    def qkv(rows):
        for i in range(3):
            part(0, rows, slice(i * D, i * D + D), own[1 + i, rows])

    def dense(rows):
        part(1, rows, slice(None), own[0, rows])

    def vectors(rows):
        part(4, slice(None), slice(None), gtable[:VROWS], vector_rate, 0.0)

    for number in order:
        for i in range(3 * number, 3 * number + 3):
            loads[i].wait()
        work = (qkv, dense, expand, shrink, vectors)[number]
        if number == 4:
            work(None)
        else:

            def some(i, carry, work=work):
                work(pl.ds(pl.multiple_of(i * 16, 16), 16))
                return carry

            lax.fori_loop(0, 8, some, 0)
        for i in range(3 * number, 3 * number + 3):
            stores[i].start()
    for i in (15, 16):
        loads[i].wait()
        stores[i].start()
    for store in stores:
        store.wait()


def update_all(norm, own, gtable, states, passed, shards):
    arrays = states + passed
    anywhere = [pl.BlockSpec(memory_space=pl.ANY)] * len(arrays)
    inside = [pl.BlockSpec(memory_space=pltpu.VMEM)] * 3

    def kernel(*refs):
        update_kernel(shards, *refs)

    new = pl.pallas_call(
        kernel,
        out_shape=tuple(jax.ShapeDtypeStruct(a.shape, a.dtype) for a in arrays),
        in_specs=inside + anywhere,
        out_specs=tuple(anywhere),
        scratch_shapes=[pltpu.VMEM(a.shape, a.dtype) for a in arrays]
        + [pltpu.SemaphoreType.DMA((len(arrays),)), pltpu.SemaphoreType.DMA((len(arrays),))],
        compiler_params=pltpu.CompilerParams(vmem_limit_bytes=56 * MIB),
        name="update",
    )(norm, own, gtable, *arrays)
    ordered = [new[3 * i + k] for i in range(5) for k in (1, 2, 0)]
    return ordered + list(new[15:])


def body(
    tokens,
    doc_lengths,
    cotangent,
    qkv_weight,
    qkv_firsts,
    qkv_seconds,
    dense_weight,
    dense_firsts,
    dense_seconds,
    expand_weight,
    expand_firsts,
    expand_seconds,
    shrink_weight,
    shrink_firsts,
    shrink_seconds,
    vectors,
    vec_firsts,
    vec_seconds,
    *,
    shards,
    reps,
):
    nz = shards // 2
    vec_own = jnp.pad(vectors.astype(BF).T, ((0, VPAD - VROWS), (0, 0)))
    full, table, ht, act, ready = front(
        doc_lengths, tokens, cotangent, qkv_weight, dense_weight, vec_own, expand_weight, shrink_weight, nz
    )
    output, grad_in, owned, gtable, norm = back(
        tokens, cotangent, ht, table, act, full.reshape(UNITS, D, D),
        ready.reshape(4, nz, 2, 2, 2, 32, D), nz, reps,
    )
    owned = owned.reshape(UNITS, 128, D)
    if reps != 4:
        quads = [[4 * i + j for i in range(reps // 4)] for j in range(4)]
        owned = lax.psum(owned, "rep", axis_index_groups=quads)
        gtable, norm = norm_all(gtable, owned, shards, reps)
    states = (
        qkv_weight, qkv_firsts, qkv_seconds,
        dense_weight, dense_firsts, dense_seconds,
        expand_weight, expand_firsts, expand_seconds,
        shrink_weight, shrink_firsts, shrink_seconds,
        vectors.T, vec_firsts.T, vec_seconds.T,
    )
    new = tuple(update_all(norm, owned, gtable, states, (output, grad_in), shards))
    return new[15:] + new[:12] + tuple(vec.T for vec in new[12:15]) + (norm.reshape(1),)


def solution(mesh):
    shards, reps = mesh.shape["shard"], mesh.shape["rep"]
    data, state = P(("rep", "shard"), None), P("shard", None)

    def step(*args):
        return body(*args, shards=shards, reps=reps)

    return jax.shard_map(
        step,
        mesh=mesh,
        in_specs=(data, data, data) + (state,) * 15,
        out_specs=(data, data) + (state,) * 15 + (P(),),
        check_vma=False,
    )
```
